512 devices in a mesh: rep: 32 (over z, y_hi, core), fsdp: 16 (over y_lo, x).
Axes of the slice: x: 4, y: 8 (y_hi: 2, y_lo: 4; y = y_hi * 4 + y_lo), z: 8, core: 2. Of those that a mesh axis runs over, the one named last changes fastest.
Arguments:
- tokens: bfloat16 [2048, 4096], P('fsdp', 'rep'), may hold values from -6 to 6
- grad_out: bfloat16 [2048, 4096], P('fsdp', 'rep'), may hold values from -6 to 6
- w_gate: bfloat16 [4096, 24576], P('fsdp', 'rep'), may hold values from -0.1875 to 0.1875
- w_up: bfloat16 [4096, 24576], P('fsdp', 'rep'), may hold values from -0.1875 to 0.1875
- w_down: bfloat16 [24576, 4096], P('rep', 'fsdp'), may hold values from -0.0390625 to 0.0390625
Outputs:
- grad_tokens: bfloat16 [2048, 4096], P('fsdp', 'rep')
- grad_gate: bfloat16 [4096, 24576], P('fsdp', 'rep')
- grad_up: bfloat16 [4096, 24576], P('fsdp', 'rep')
- grad_down: bfloat16 [24576, 4096], P('rep', 'fsdp')
The draws below stay inside these ranges and needn't reach their ends.
All inputs are finite; a program needn't handle non-finite values.
Results may differ from the reference program's by a relative error of at most 0.0049.
Values may be sent and summed in bfloat16 or wider, within the bound.
No kernel may reach another device: no remote copies, remote signals or barrier semaphores. Data moves between devices by JAX's collectives and lax.ppermute only.
A program may use at most 64 MiB of HBM per device.

```python
import math
import jax
import jax.numpy as jnp
from jax import lax

D = 4096
FF = 24576
HB = 128
TOKENS = 2048


def raised(entries, key, source, target, blocks, factor):
    owner, partner = [(jnp.arange(entries.shape[dim]) // (entries.shape[dim] // blocks)).reshape([-1 if axis == dim else 1 for axis in range(entries.ndim)]) for dim in (source, target)]
    chosen = jax.random.permutation(key, blocks)[partner]
    strong = (owner == chosen) | (owner == (partner + blocks // 2) % blocks)
    return jnp.where(strong, factor * entries, entries)


def block_levels(own_key, shape, cuts, smallest, high):
    def one(dim, blocks):
        draws = jax.random.uniform(jax.random.fold_in(jax.random.fold_in(own_key, 6), dim), (blocks,), jnp.float32, smallest / len(cuts), high / len(cuts))
        return jnp.repeat(jnp.exp(draws), shape[dim] // blocks).reshape((-1,) + (1,) * (len(shape) - dim - 1))

    gain = one(*cuts[0])
    for cut in cuts[1:]:
        gain = gain * one(*cut)
    return gain


def scatter_about(key, dims, deviation, reach, shards=(), kind=jnp.bfloat16):
    loudness = block_levels(key, dims, shards, -0.22, 0.18) if shards else 1.0
    array = jax.random.normal(key, dims, jnp.float32) * deviation * loudness
    return jnp.minimum(jnp.maximum(array, -reach), reach).astype(kind)


def noise_with(key, shape, deviation, bound, shards, heavy, kind=jnp.bfloat16):
    entries = deviation * jax.random.normal(key, shape, jnp.float32)
    if shards:
        entries = entries * block_levels(key, shape, shards, -0.22, 0.18)
    return jnp.clip(raised(entries, jax.random.fold_in(key, 3), *heavy), -bound, bound).astype(kind)


def setup_inputs(seed: int = 0) -> dict:
    key_list = jax.random.split(jax.random.key(seed), 6)
    return {
        "tokens": scatter_about(key_list[0], (TOKENS, D), 1.0, 6.0, ((0, 16), (1, 32))),
        "grad_out": scatter_about(key_list[1], (TOKENS, D), 1.0, 6.0, ((0, 16), (1, 32))),
        "w_gate": noise_with(key_list[2], (D, FF), D ** -0.5, 0.1875, ((0, 16), (1, 32)), (1, 0, 32, 2.75)),
        "w_up": noise_with(key_list[3], (D, FF), D ** -0.5, 0.1875, ((0, 16), (1, 32)), (1, 0, 32, 2.75)),
        "w_down": scatter_about(key_list[4], (FF, D), FF ** -0.5, 0.0390625, ((0, 32), (1, 16))),
    }


def hadamard(size):
    index = jnp.arange(size, dtype=jnp.int32)
    both = index[:, None] & index[None, :]
    parity = jnp.zeros((size, size), jnp.int32)
    for bit_pos in range(size.bit_length() - 1):
        parity = parity + (both >> bit_pos & 1)
    return (1 - 2 * (parity % 2)).astype(jnp.float32) / math.sqrt(size)

def reference(tokens, grad_out, w_gate, w_up, w_down):
    gate = jnp.dot(tokens, w_gate, preferred_element_type=jnp.float32)
    up = jnp.dot(tokens, w_up, preferred_element_type=jnp.float32)
    sig = jax.nn.sigmoid(gate)
    active = gate * sig
    hidden = (active * up).astype(jnp.bfloat16)
    d_hidden = jnp.dot(grad_out, w_down.T, preferred_element_type=jnp.float32)
    d_gate = (d_hidden * up * sig * (1.0 + gate * (1.0 - sig))).astype(jnp.bfloat16)
    d_up = (d_hidden * active).astype(jnp.bfloat16)
    grad_tokens = (jnp.dot(d_gate, w_gate.T, preferred_element_type=jnp.float32) + jnp.dot(d_up, w_up.T, preferred_element_type=jnp.float32)).astype(jnp.bfloat16)
    gw_gate = jnp.dot(tokens.T, d_gate, preferred_element_type=jnp.float32)
    gw_up = jnp.dot(tokens.T, d_up, preferred_element_type=jnp.float32)
    gw_down = jnp.dot(hidden.T, grad_out, preferred_element_type=jnp.float32)
    rotor = hadamard(HB)

    def rotate_rows(grad):
        blocks = grad.reshape(D // HB, HB, FF)
        return jnp.einsum('ij,bjf->bif', rotor, blocks, precision=lax.Precision.HIGHEST).reshape(D, FF).astype(jnp.bfloat16)
    blocks = gw_down.reshape(FF, D // HB, HB)
    grad_down = jnp.einsum('fbj,ij->fbi', blocks, rotor, precision=lax.Precision.HIGHEST).reshape(FF, D).astype(jnp.bfloat16)
    return (grad_tokens, rotate_rows(gw_gate), rotate_rows(gw_up), grad_down)
```

```python
import math

import jax
import jax.numpy as jnp
from jax import lax
from jax.sharding import Mesh
from jax.sharding import PartitionSpec as P

HB = 128
CHUNKS = 1
SIZES = {"z": 8, "h": 2, "c": 2, "y": 4, "x": 4}
EVERY = ("z", "h", "c", "y", "x")
REP = ("z", "h", "c")
FSDP = ("y", "x")
BF = jnp.bfloat16
F32 = jnp.float32


def hadamard(size):
    index = jnp.arange(size, dtype=jnp.int32)
    both = index[:, None] & index[None, :]
    parity = jnp.zeros((size, size), jnp.int32)
    for bit_pos in range(size.bit_length() - 1):
        parity = parity + (both >> bit_pos & 1)
    return (1 - 2 * (parity % 2)).astype(F32) / math.sqrt(size)


def exchange_pairs():
    nz, nh, nc, ny, nx = (SIZES[a] for a in EVERY)
    pairs = []
    for z in range(nz):
        for h in range(nh):
            for c in range(nc):
                for y in range(ny):
                    for x in range(nx):
                        tail = (h * nc + c) * ny
                        src = ((z * nh * nc * ny) + tail + y) * nx + x
                        zz, yy = 2 * y + z % 2, z // 2
                        dst = ((zz * nh * nc * ny) + tail + yy) * nx + x
                        pairs.append((src, dst))
    return pairs


def dot(left, right, dims):
    return lax.dot_general(left, right, (dims, ((), ())), preferred_element_type=F32)


def swap_all_to_all(value, axes):
    return lax.all_to_all(value, axes, split_axis=0, concat_axis=0, tiled=True)


def gather_tokens(tokens, grad_out):
    ny = SIZES["y"]
    t, d = tokens.shape
    both = jnp.stack([tokens, grad_out])
    both = lax.ppermute(both, EVERY, exchange_pairs())
    ways = SIZES["z"] * SIZES["h"]
    mine = lax.all_to_all(
        jnp.broadcast_to(both[None], (ways,) + both.shape), ("z", "h"), 0, 0, tiled=True
    )
    other = lax.ppermute(mine, "c", [(0, 1), (1, 0)])
    first = lax.axis_index("c") == 0
    lo, hi = jnp.where(first, mine, other), jnp.where(first, other, mine)
    parts = [v.reshape(ny, ways // ny, 2, t, d) for v in (lo, hi)]
    out = []
    for s in range(2):
        one = jnp.stack([p[:, :, s] for p in parts], axis=2)
        out.append(one.transpose(0, 3, 1, 2, 4).reshape(ny * t, -1))
    return out


def body(tokens, grad_out, w_gate, w_up, w_down):
    nx, ny = SIZES["x"], SIZES["y"]
    rows, cols = w_gate.shape
    width = cols // CHUNKS
    w_down_t = w_down.T
    weights = []
    for k in range(CHUNKS):
        part = slice(k * width, (k + 1) * width)
        own = jnp.concatenate([w_gate[:, part], w_up[:, part], w_down_t[:, part]], axis=1)
        weights.append(lax.all_gather(own, "x", axis=0, tiled=True))
    x2, dy2 = gather_tokens(tokens, grad_out)
    t = tokens.shape[0]
    rotor = hadamard(HB)

    grad_x = None
    gates, ups, downs = [], [], []
    for k in range(CHUNKS):
        w = weights[k]
        gu = dot(x2, w[:, : 2 * width], ((1,), (0,))).astype(BF)
        dh = dot(dy2, w[:, 2 * width :], ((1,), (0,))).astype(BF)
        gu = swap_all_to_all(gu.reshape(ny, t, 2 * width), "y")
        dh = swap_all_to_all(dh.reshape(ny, t, width), "y")
        gu = jnp.sum(gu.astype(F32), axis=0)
        d_hidden = jnp.sum(dh.astype(F32), axis=0)
        gate, up = gu[:, :width], gu[:, width:]
        sig = jax.nn.sigmoid(gate)
        active = gate * sig
        hidden = (active * up).astype(BF)
        d_gate = (d_hidden * up * sig * (1.0 + gate * (1.0 - sig))).astype(BF)
        d_up = (d_hidden * active).astype(BF)
        full = lax.all_gather(
            jnp.concatenate([d_gate, d_up, hidden], axis=1), "y", axis=0, tiled=True
        )
        dgu, hid = full[:, : 2 * width], full[:, 2 * width :]
        gw = jnp.concatenate(
            [
                dot(x2, dgu, ((0,), (0,))).astype(BF),
                dot(dy2, hid, ((0,), (0,))).astype(BF),
            ],
            axis=1,
        )
        gw = swap_all_to_all(gw.reshape(nx, rows, 3 * width), "x")
        part_x = dot(dgu, w[:, : 2 * width], ((1,), (1,)))
        grad_x = part_x if grad_x is None else grad_x + part_x
        gw = jnp.sum(gw.astype(F32), axis=0).reshape(rows // HB, HB, 3, width)
        rot = jnp.einsum(
            "ij,bjsf->sbif", rotor, gw[:, :, :2], precision=lax.Precision.HIGHEST
        ).astype(BF)
        gates.append(rot[0].reshape(rows, width))
        ups.append(rot[1].reshape(rows, width))
        downs.append(
            jnp.einsum("bjf,ij->fbi", gw[:, :, 2], rotor, precision=lax.Precision.HIGHEST)
            .reshape(width, rows)
            .astype(BF)
        )

    d = tokens.shape[1]
    spread = grad_x.shape[1] // d
    pieces = grad_x.reshape(ny, t, spread, d).transpose(0, 2, 1, 3).reshape(-1, t, d)
    pieces = swap_all_to_all(pieces.astype(BF), REP)
    grad_tokens = jnp.sum(pieces.astype(F32), axis=0).astype(BF)
    grad_tokens = lax.ppermute(grad_tokens, EVERY, exchange_pairs())
    return (
        grad_tokens,
        jnp.concatenate(gates, axis=1),
        jnp.concatenate(ups, axis=1),
        jnp.concatenate(downs, axis=0),
    )


def solution(mesh):
    fine = Mesh(mesh.devices.reshape(tuple(SIZES[a] for a in EVERY)), EVERY)
    return jax.shard_map(
        body,
        mesh=fine,
        in_specs=(P(FSDP, REP), P(FSDP, REP), P(FSDP, REP), P(FSDP, REP), P(REP, FSDP)),
        out_specs=(P(FSDP, REP), P(FSDP, REP), P(FSDP, REP), P(REP, FSDP)),
        check_vma=False,
    )
```

```python
import math

import jax
import jax.numpy as jnp
from jax import lax
from jax.sharding import Mesh
from jax.sharding import PartitionSpec as P

HB = 128
CHUNKS = 2
SIZES = {"z": 8, "h": 2, "c": 2, "y": 4, "x": 4}
EVERY = ("z", "h", "c", "y", "x")
REP = ("z", "h", "c")
FSDP = ("y", "x")
BF = jnp.bfloat16
F32 = jnp.float32


def hadamard(size):
    index = jnp.arange(size, dtype=jnp.int32)
    both = index[:, None] & index[None, :]
    parity = jnp.zeros((size, size), jnp.int32)
    for bit_pos in range(size.bit_length() - 1):
        parity = parity + (both >> bit_pos & 1)
    return (1 - 2 * (parity % 2)).astype(F32) / math.sqrt(size)


def exchange_pairs(flip):
    nz, nh, nc, ny, nx = (SIZES[a] for a in EVERY)
    pairs = []
    for z in range(nz):
        for h in range(nh):
            for c in range(nc):
                for y in range(ny):
                    for x in range(nx):
                        src = (((z * nh + h) * nc + c) * ny + y) * nx + x
                        zz, yy, hh = 2 * y + z % 2, z // 2, h ^ flip
                        dst = (((zz * nh + hh) * nc + c) * ny + yy) * nx + x
                        pairs.append((src, dst))
    return pairs


def dot(left, right, dims):
    return lax.dot_general(left, right, (dims, ((), ())), preferred_element_type=F32)


def swap_all_to_all(value, axes):
    return lax.all_to_all(value, axes, split_axis=0, concat_axis=0, tiled=True)


def gather_all_to_all(value, axes, ways):
    return swap_all_to_all(jnp.broadcast_to(value[None], (ways,) + value.shape), axes)


def sum_first(value):
    terms = [value[i].astype(F32) for i in range(value.shape[0])]
    while len(terms) > 1:
        terms = [a + b for a, b in zip(terms[::2], terms[1::2])]
    return terms[0]


def other_core(value):
    return lax.ppermute(value, "c", [(0, 1), (1, 0)])


def gather_tokens(tokens, grad_out):
    nz, ny = SIZES["z"], SIZES["y"]
    t, d = tokens.shape
    both = jnp.stack([tokens, grad_out])
    mine = lax.ppermute(both, EVERY, exchange_pairs(0))
    far = lax.ppermute(both, EVERY, exchange_pairs(1))
    low = lax.axis_index("h") == 0
    first = lax.axis_index("c") == 0
    out = []
    for s in range(2):
        pair = jnp.stack(
            [jnp.where(low, mine[s], far[s]), jnp.where(low, far[s], mine[s])]
        )
        one = gather_all_to_all(pair, "z", nz)
        other = other_core(one)
        one = jnp.stack([jnp.where(first, one, other), jnp.where(first, other, one)], axis=2)
        one = one.reshape(ny, -1, t, d).transpose(0, 2, 1, 3)
        out.append(one.reshape(ny * t, -1))
    return out


def exchange_sum(value, axis):
    n = value.shape[0]
    me = lax.axis_index(axis)

    def block(i):
        return lax.dynamic_index_in_dim(value, i, 0, keepdims=False)

    terms = [block(me)]
    for step in (1, n - 1, *range(2, n - 1)):
        pairs = [(i, (i + step) % n) for i in range(n)]
        terms.append(lax.ppermute(block((me + step) % n), axis, pairs))
    total = terms[0].astype(F32)
    for term in terms[1:]:
        total = total + term.astype(F32)
    return total


def scatter_grad_tokens(grad_x, t, d):
    ny = SIZES["y"]
    pieces = grad_x.reshape(ny, t, -1, 2, d).transpose(3, 0, 2, 1, 4)
    core = lax.axis_index("c")
    keep = lax.dynamic_index_in_dim(pieces, core, 0, keepdims=False)
    give = lax.dynamic_index_in_dim(pieces, 1 - core, 0, keepdims=False)
    pieces = (keep + other_core(give)).astype(BF).reshape(-1, t, d)
    pieces = swap_all_to_all(pieces, ("z", "h"))
    return lax.ppermute(sum_first(pieces).astype(BF), EVERY, exchange_pairs(0))


def body(tokens, grad_out, w_gate, w_up, w_down):
    nx, ny = SIZES["x"], SIZES["y"]
    rows, cols = w_gate.shape
    width = cols // CHUNKS
    w_down_t = w_down.T
    weights = []
    for k in range(CHUNKS):
        part = slice(k * width, (k + 1) * width)
        own = jnp.concatenate([w_gate[:, part], w_up[:, part], w_down_t[:, part]], axis=1)
        weights.append(lax.all_gather(own, "x", axis=0, tiled=True))
    x2, dy2 = gather_tokens(tokens, grad_out)
    t, d = tokens.shape
    rotor = hadamard(HB)

    grad_x = None
    gates, ups, downs = [], [], []
    for k in range(CHUNKS):
        w = weights[k]
        gu = dot(x2, w[:, : 2 * width], ((1,), (0,))).astype(BF)
        dh = dot(dy2, w[:, 2 * width :], ((1,), (0,))).astype(BF)
        gu = sum_first(swap_all_to_all(gu.reshape(ny, t, 2 * width), "y"))
        d_hidden = sum_first(swap_all_to_all(dh.reshape(ny, t, width), "y"))
        gate, up = gu[:, :width], gu[:, width:]
        sig = jax.nn.sigmoid(gate)
        active = gate * sig
        hidden = (active * up).astype(BF)
        d_gate = (d_hidden * up * sig * (1.0 + gate * (1.0 - sig))).astype(BF)
        d_up = (d_hidden * active).astype(BF)
        full = gather_all_to_all(
            jnp.concatenate([d_gate, d_up, hidden], axis=1), "y", ny
        ).reshape(ny * t, 3 * width)
        dgu, hid = full[:, : 2 * width], full[:, 2 * width :]
        part_x = dot(dgu, w[:, : 2 * width], ((1,), (1,)))
        grad_x = part_x if grad_x is None else grad_x + part_x
        gw = jnp.concatenate(
            [
                dot(x2, dgu, ((0,), (0,))).astype(BF),
                dot(dy2, hid, ((0,), (0,))).astype(BF),
            ],
            axis=1,
        )
        gw = exchange_sum(gw.reshape(nx, rows, 3 * width), "x")
        gw = gw.reshape(rows // HB, HB, 3 * width)
        rot = jnp.einsum(
            "ij,bjf->bif", rotor, gw[:, :, : 2 * width], precision=lax.Precision.HIGHEST
        ).astype(BF)
        rot = rot.reshape(rows, 2 * width)
        gates.append(rot[:, :width])
        ups.append(rot[:, width:])
        downs.append(
            jnp.einsum(
                "bjf,ij->fbi", gw[:, :, 2 * width :], rotor, precision=lax.Precision.HIGHEST
            )
            .reshape(width, rows)
            .astype(BF)
        )
    return (
        scatter_grad_tokens(grad_x, t, d),
        jnp.concatenate(gates, axis=1),
        jnp.concatenate(ups, axis=1),
        jnp.concatenate(downs, axis=0),
    )


def solution(mesh):
    fine = Mesh(mesh.devices.reshape(tuple(SIZES[a] for a in EVERY)), EVERY)
    return jax.shard_map(
        body,
        mesh=fine,
        in_specs=(P(FSDP, REP), P(FSDP, REP), P(FSDP, REP), P(FSDP, REP), P(REP, FSDP)),
        out_specs=(P(FSDP, REP), P(FSDP, REP), P(FSDP, REP), P(REP, FSDP)),
        check_vma=False,
    )
```

```python
import math

import jax
import jax.numpy as jnp
from jax import lax
from jax.sharding import Mesh
from jax.sharding import PartitionSpec as P

HB = 128
WIDTHS = (384, 384)
SIZES = {"z": 8, "h": 2, "c": 2, "y": 4, "x": 4}
EVERY = ("z", "h", "c", "y", "x")
REP = ("z", "h", "c")
FSDP = ("y", "x")
BF = jnp.bfloat16
F32 = jnp.float32


def hadamard(size):
    index = jnp.arange(size, dtype=jnp.int32)
    both = index[:, None] & index[None, :]
    parity = jnp.zeros((size, size), jnp.int32)
    for bit_pos in range(size.bit_length() - 1):
        parity = parity + (both >> bit_pos & 1)
    return (1 - 2 * (parity % 2)).astype(F32) / math.sqrt(size)


def exchange_pairs(flip, back=False):
    nz, nh, nc, ny, nx = (SIZES[a] for a in EVERY)
    pairs = []
    for z in range(nz):
        for h in range(nh):
            for c in range(nc):
                for y in range(ny):
                    for x in range(nx):
                        src = (((z * nh + h) * nc + c) * ny + y) * nx + x
                        yy, hh = z // 2, h ^ flip
                        zz = 2 * (y ^ yy) + z % 2
                        dst = (((zz * nh + hh) * nc + c) * ny + yy) * nx + x
                        pairs.append((dst, src) if back else (src, dst))
    return pairs


def dot(left, right, dims):
    return lax.dot_general(left, right, (dims, ((), ())), preferred_element_type=F32)


def swap_all_to_all(value, axes):
    return lax.all_to_all(value, axes, split_axis=0, concat_axis=0, tiled=True)


def sum_first(value):
    terms = [value[i].astype(F32) for i in range(value.shape[0])]
    while len(terms) > 1:
        terms = [a + b for a, b in zip(terms[::2], terms[1::2])]
    return terms[0]


def other_core(value):
    return lax.ppermute(value, "c", [(0, 1), (1, 0)])


def gather_tokens(tokens, grad_out):
    nz, ny = SIZES["z"], SIZES["y"]
    t, d = tokens.shape
    both = jnp.stack([tokens, grad_out])
    mine = lax.ppermute(both, EVERY, exchange_pairs(0))
    far = lax.ppermute(both, EVERY, exchange_pairs(1))
    low = lax.axis_index("h") == 0
    first = lax.axis_index("c") == 0
    pair = jnp.stack([jnp.where(low, mine, far), jnp.where(low, far, mine)])
    one = swap_all_to_all(jnp.broadcast_to(pair[None], (nz,) + pair.shape), "z")
    other = other_core(one)
    one, other = jnp.where(first, one, other), jnp.where(first, other, one)
    out = []
    for s in range(2):
        part = jnp.stack([one[:, :, s], other[:, :, s]], axis=2)
        part = part.reshape(ny, -1, t, d).transpose(0, 2, 1, 3)
        out.append(part.reshape(ny, t, -1))
    return out


def after(value, others):
    return value if others is None else lax.optimization_barrier((value, others))[0]


def trade(blocks, axis, partners):
    return [lax.ppermute(b, axis, p) for b, p in zip(blocks, partners)]


def split_grad_tokens(grad_x, t, d):
    pieces = grad_x.reshape(SIZES["y"], t, -1, 2, d).transpose(3, 0, 2, 1, 4)
    first = lax.axis_index("c") == 0
    return (
        jnp.where(first, pieces[0], pieces[1]),
        jnp.where(first, pieces[1], pieces[0]),
    )


def scatter_grad_tokens(pieces):
    pieces = swap_all_to_all(pieces, ("z", "h"))
    return lax.ppermute(sum_first(pieces).astype(BF), EVERY, exchange_pairs(0, True))


def body(tokens, grad_out, w_gate, w_up, w_down):
    nx, ny = SIZES["x"], SIZES["y"]
    rows = w_gate.shape[0]
    t, d = tokens.shape
    y_partners = [[(i, i ^ k) for i in range(ny)] for k in range(1, ny)]
    x_partners = [[(i, (i + k) % nx) for i in range(nx)] for k in (1, nx - 1, 2)]
    w_down_t = w_down.T
    weights = []
    at = 0
    for width in WIDTHS:
        part = slice(at, at + width)
        at += width
        own = jnp.concatenate([w_gate[:, part], w_up[:, part], w_down_t[:, part]], axis=1)
        weights.append(lax.all_gather(own, "x", axis=0, tiled=True))
    x2, dy2 = gather_tokens(tokens, grad_out)
    rotor = hadamard(HB)
    me = lax.axis_index("x")

    shares = []
    done = None
    for w, width in zip(weights, WIDTHS):
        w = after(w, done)

        def share(k):
            gu = dot(x2[k], w[:, : 2 * width], ((1,), (0,)))
            dh = dot(dy2[k], w[:, 2 * width :], ((1,), (0,)))
            return gu, dh
        send = [jnp.concatenate([v.astype(BF) for v in share(k)], axis=1) for k in range(1, ny)]
        got = trade(send, "y", y_partners)
        done = got[0]
        shares.append((share(0), got))

    fulls = []
    for ((gu, d_hidden), others), width in zip(shares, WIDTHS):
        for o in others:
            gu = gu + o[:, : 2 * width].astype(F32)
            d_hidden = d_hidden + o[:, 2 * width :].astype(F32)
        gate, up = gu[:, :width], gu[:, width:]
        sig = jax.nn.sigmoid(gate)
        active = gate * sig
        hidden = (active * up).astype(BF)
        d_gate = (d_hidden * up * sig * (1.0 + gate * (1.0 - sig))).astype(BF)
        d_up = (d_hidden * active).astype(BF)
        mine = jnp.concatenate([d_gate, d_up, hidden], axis=1)
        fulls.append(jnp.concatenate([mine, *trade([mine] * (ny - 1), "y", y_partners)], axis=0))

    def columns(v, step):
        v = v.reshape(ny * t, -1)
        return lax.dynamic_slice_in_dim(v, lax.rem(me + step, nx) * rows, rows, axis=1)

    steps = (0, 1, nx - 1, 2)
    x_cols = [columns(x2, s) for s in steps]
    dy_cols = [columns(dy2, s) for s in steps]
    grad_x = 0.0
    sums = []
    done = None
    for full, w, width in zip(fulls, weights, WIDTHS):
        full = after(full, done)
        grad_x = grad_x + dot(full[:, : 2 * width], w[:, : 2 * width], ((1,), (1,)))
        if len(sums) == len(WIDTHS) - 1:
            keep, give = split_grad_tokens(grad_x, t, d)
            full = after(full, give)

        def piece(k):
            return jnp.concatenate(
                [
                    dot(x_cols[k], full[:, : 2 * width], ((0,), (0,))),
                    dot(dy_cols[k], full[:, 2 * width :], ((0,), (0,))),
                ],
                axis=1,
            )

        send = [piece(k).astype(BF) for k in range(1, nx)]
        done = got = trade(send, "x", x_partners)
        sums.append((piece(0), got))
    pieces = (keep + other_core(give)).astype(BF).reshape(-1, t, d)
    grad_tokens = scatter_grad_tokens(pieces)

    gates, ups, downs = [], [], []
    for (gw, got), width in zip(sums, WIDTHS):
        gw = after(gw, pieces if got is done else send)
        for g in got:
            gw = gw + g.astype(F32)
        gw = gw.reshape(rows // HB, HB, 3 * width)
        rot = jnp.einsum(
            "ij,bjf->bif", rotor, gw[:, :, : 2 * width], precision=lax.Precision.HIGHEST
        ).astype(BF)
        rot = rot.reshape(rows, 2 * width)
        gates.append(rot[:, :width])
        ups.append(rot[:, width:])
        downs.append(
            jnp.einsum(
                "bjf,ij->fbi", gw[:, :, 2 * width :], rotor, precision=lax.Precision.HIGHEST
            )
            .reshape(width, rows)
            .astype(BF)
        )
    return (
        grad_tokens,
        jnp.concatenate(gates, axis=1),
        jnp.concatenate(ups, axis=1),
        jnp.concatenate(downs, axis=0),
    )


def solution(mesh):
    fine = Mesh(mesh.devices.reshape(tuple(SIZES[a] for a in EVERY)), EVERY)
    return jax.shard_map(
        body,
        mesh=fine,
        in_specs=(P(FSDP, REP), P(FSDP, REP), P(FSDP, REP), P(FSDP, REP), P(REP, FSDP)),
        out_specs=(P(FSDP, REP), P(FSDP, REP), P(FSDP, REP), P(REP, FSDP)),
        check_vma=False,
    )
```

```python
import math

import jax
import jax.numpy as jnp
from jax import lax
from jax.sharding import Mesh
from jax.sharding import PartitionSpec as P

HB = 128
WIDTHS = (384, 384)
SIZES = {"z": 8, "h": 2, "c": 2, "y": 4, "x": 4}
EVERY = ("z", "h", "c", "y", "x")
REP = ("z", "h", "c")
FSDP = ("y", "x")
BF = jnp.bfloat16
F32 = jnp.float32


def hadamard(size):
    index = jnp.arange(size, dtype=jnp.int32)
    both = index[:, None] & index[None, :]
    parity = jnp.zeros((size, size), jnp.int32)
    for bit_pos in range(size.bit_length() - 1):
        parity = parity + (both >> bit_pos & 1)
    return (1 - 2 * (parity % 2)).astype(F32) / math.sqrt(size)


ORDER = (0, 2, 1, 3)


def exchange_pairs(flip, back=False):
    nz, nh, nc, ny, nx = (SIZES[a] for a in EVERY)
    pairs = []
    for z in range(nz):
        for h in range(nh):
            for c in range(nc):
                for y in range(ny):
                    for x in range(nx):
                        src = (((z * nh + h) * nc + c) * ny + y) * nx + x
                        yy, hh = z // 2, h ^ flip
                        zz = 2 * ORDER[y ^ yy] + z % 2
                        dst = (((zz * nh + hh) * nc + c) * ny + yy) * nx + x
                        pairs.append((dst, src) if back else (src, dst))
    return pairs


def dot(left, right, dims):
    return lax.dot_general(left, right, (dims, ((), ())), preferred_element_type=F32)


def swap_all_to_all(value, axes):
    return lax.all_to_all(value, axes, split_axis=0, concat_axis=0, tiled=True)


def sum_first(value):
    terms = [value[i].astype(F32) for i in range(value.shape[0])]
    while len(terms) > 1:
        terms = [a + b for a, b in zip(terms[::2], terms[1::2])]
    return terms[0]


def other_core(value):
    return lax.ppermute(value, "c", [(0, 1), (1, 0)])


def gather_tokens(tokens, grad_out):
    nz, ny = SIZES["z"], SIZES["y"]
    t, d = tokens.shape
    both = jnp.stack([tokens, grad_out])
    mine = lax.ppermute(both, EVERY, exchange_pairs(0))
    far = lax.ppermute(both, EVERY, exchange_pairs(1))
    low = lax.axis_index("h") == 0
    first = lax.axis_index("c") == 0
    out = []
    for s in range(2):
        pair = jnp.stack([jnp.where(low, mine[s], far[s]), jnp.where(low, far[s], mine[s])])
        pair = jnp.broadcast_to(pair[None], (nz,) + pair.shape)
        if out:
            pair = after(pair, one)
        one = swap_all_to_all(pair, "z")
        other = other_core(one)
        part = jnp.stack([jnp.where(first, one, other), jnp.where(first, other, one)], axis=2)
        out.append(part.reshape(ny, -1, t, d).transpose(0, 2, 1, 3).reshape(ny * t, -1))
    return out


def after(value, others):
    return value if others is None else lax.optimization_barrier((value, others))[0]


def trade(blocks, axis, partners):
    return [lax.ppermute(b, axis, p) for b, p in zip(blocks, partners)]


def xor_trade(value, step):
    return lax.ppermute(value, "y", [(i, i ^ step) for i in range(SIZES["y"])])


def scatter_grad_tokens(pieces):
    pieces = swap_all_to_all(pieces, ("z", "h"))
    return lax.ppermute(sum_first(pieces).astype(BF), EVERY, exchange_pairs(0, True))


def body(tokens, grad_out, w_gate, w_up, w_down):
    nx, ny = SIZES["x"], SIZES["y"]
    rows = w_gate.shape[0]
    t, d = tokens.shape
    x_partners = [[(i, (i + k) % nx) for i in range(nx)] for k in (1, nx - 1, 2)]
    w_down_t = w_down.T
    weights = []
    at = 0
    for width in WIDTHS:
        part = slice(at, at + width)
        at += width
        own = jnp.concatenate([w_gate[:, part], w_up[:, part], w_down_t[:, part]], axis=1)
        weights.append(lax.all_gather(own, "x", axis=0, tiled=True))
    x2, dy2 = gather_tokens(tokens, grad_out)
    rotor = hadamard(HB)
    me = lax.axis_index("x")

    half = 2 * t
    kept, fulls = [], []
    done = None
    for w, width in zip(weights, WIDTHS):
        w = after(w, done)
        cut = 2 * width
        sides = [(x2, w[:, :cut]), (dy2, w[:, cut:])]
        give = [dot(v[half:], u, ((1,), (0,))).astype(BF) for v, u in sides]
        if kept:
            got = [xor_trade(jnp.concatenate(give, axis=1), 1)]
            got = [got[0][:, :cut], got[0][:, cut:]]
        else:
            got = [xor_trade(g, 1) for g in give]
        keep = [dot(v[:half], u, ((1,), (0,))) for v, u in sides]
        keep = [k + g.astype(F32) for k, g in zip(keep, got)]
        done = jnp.concatenate([k[t:].astype(BF) for k in keep], axis=1)
        kept.append(([k[:t] for k in keep], xor_trade(done, 2)))

    for ((gu, d_hidden), got), width in zip(kept, WIDTHS):
        gu = gu + got[:, : 2 * width].astype(F32)
        d_hidden = d_hidden + got[:, 2 * width :].astype(F32)
        gate, up = gu[:, :width], gu[:, width:]
        sig = jax.nn.sigmoid(gate)
        active = gate * sig
        hidden = (active * up).astype(BF)
        d_gate = (d_hidden * up * sig * (1.0 + gate * (1.0 - sig))).astype(BF)
        d_up = (d_hidden * active).astype(BF)
        mine = jnp.concatenate([d_gate, d_up, hidden], axis=1)
        mine = jnp.concatenate([mine, xor_trade(mine, 2)], axis=0)
        fulls.append(jnp.concatenate([mine, xor_trade(mine, 1)], axis=0))

    def columns(v, step):
        return lax.dynamic_slice_in_dim(v, lax.rem(me + step, nx) * rows, rows, axis=1)

    steps = (0, 1, nx - 1, 2)
    x_cols = [columns(x2, s) for s in steps]
    dy_cols = [columns(dy2, s) for s in steps]

    first = lax.axis_index("c") == 0

    def core_rows(w, own):
        w = w.reshape(-1, 2, d, w.shape[1])
        return jnp.where(first == own, w[:, 0], w[:, 1]).reshape(-1, w.shape[-1])

    sums = []
    give = keep = 0.0
    done = None
    for full, w, width in zip(fulls, weights, WIDTHS):
        full = after(full, done)
        dgu, hid = full[:, : 2 * width], full[:, 2 * width :]
        give = give + dot(dgu, core_rows(w[:, : 2 * width], False), ((1,), (1,)))
        if len(sums) == len(WIDTHS) - 1:
            dgu, hid = after((dgu, hid), give)

        def piece(k):
            return jnp.concatenate(
                [dot(x_cols[k], dgu, ((0,), (0,))), dot(dy_cols[k], hid, ((0,), (0,)))], axis=1
            )

        send = [piece(k).astype(BF) for k in range(1, nx)]
        got = trade(send, "x", x_partners)
        done = got[0]
        keep = keep + dot(dgu, core_rows(w[:, : 2 * width], True), ((1,), (1,)))
        sums.append((piece(0), got))
    pieces = (keep + other_core(give)).astype(BF).reshape(ny, t, -1, d)
    pieces = pieces.transpose(0, 2, 1, 3).reshape(-1, t, d)
    grad_tokens = scatter_grad_tokens(pieces)

    gates, ups, downs = [], [], []
    for (gw, got), width in zip(sums, WIDTHS):
        gw = after(gw, pieces if got[0] is done else send)
        for g in got:
            gw = gw + g.astype(F32)
        gw = gw.reshape(rows // HB, HB, 3 * width)
        rot = jnp.einsum(
            "ij,bjf->bif", rotor, gw[:, :, : 2 * width], precision=lax.Precision.HIGHEST
        ).astype(BF)
        rot = rot.reshape(rows, 2 * width)
        gates.append(rot[:, :width])
        ups.append(rot[:, width:])
        downs.append(
            jnp.einsum(
                "bjf,ij->fbi", gw[:, :, 2 * width :], rotor, precision=lax.Precision.HIGHEST
            )
            .reshape(width, rows)
            .astype(BF)
        )
    return (
        grad_tokens,
        jnp.concatenate(gates, axis=1),
        jnp.concatenate(ups, axis=1),
        jnp.concatenate(downs, axis=0),
    )


def solution(mesh):
    fine = Mesh(mesh.devices.reshape(tuple(SIZES[a] for a in EVERY)), EVERY)
    return jax.shard_map(
        body,
        mesh=fine,
        in_specs=(P(FSDP, REP), P(FSDP, REP), P(FSDP, REP), P(FSDP, REP), P(REP, FSDP)),
        out_specs=(P(FSDP, REP), P(FSDP, REP), P(FSDP, REP), P(REP, FSDP)),
        check_vma=False,
    )
```

```python
import math

import jax
import jax.numpy as jnp
from jax import lax
from jax.sharding import Mesh
from jax.sharding import PartitionSpec as P

HB = 128
WIDTHS = (384, 384)
SIZES = {"z": 8, "h": 2, "c": 2, "y": 4, "x": 4}
EVERY = ("z", "h", "c", "y", "x")
REP = ("z", "h", "c")
FSDP = ("y", "x")
BF = jnp.bfloat16
F32 = jnp.float32


def hadamard(size):
    index = jnp.arange(size, dtype=jnp.int32)
    both = index[:, None] & index[None, :]
    parity = jnp.zeros((size, size), jnp.int32)
    for bit_pos in range(size.bit_length() - 1):
        parity = parity + (both >> bit_pos & 1)
    return (1 - 2 * (parity % 2)).astype(F32) / math.sqrt(size)


ORDER = (0, 2, 1, 3)


def exchange_pairs(flip, back=False):
    nz, nh, nc, ny, nx = (SIZES[a] for a in EVERY)
    pairs = []
    for z in range(nz):
        for h in range(nh):
            for c in range(nc):
                for y in range(ny):
                    for x in range(nx):
                        src = (((z * nh + h) * nc + c) * ny + y) * nx + x
                        yy, hh = z // 2, h ^ flip
                        zz = 2 * ORDER[y ^ yy] + z % 2
                        dst = (((zz * nh + hh) * nc + c) * ny + yy) * nx + x
                        pairs.append((dst, src) if back else (src, dst))
    return pairs


def dot(left, right, dims):
    return lax.dot_general(left, right, (dims, ((), ())), preferred_element_type=F32)


def swap_all_to_all(value, axes):
    return lax.all_to_all(value, axes, split_axis=0, concat_axis=0, tiled=True)


def sum_first(value):
    terms = [value[i].astype(F32) for i in range(value.shape[0])]
    while len(terms) > 1:
        terms = [a + b for a, b in zip(terms[::2], terms[1::2])]
    return terms[0]


def other_core(value):
    return lax.ppermute(value, "c", [(0, 1), (1, 0)])


def gather_tokens(tokens, grad_out):
    nz = SIZES["z"]
    both = jnp.stack([tokens, grad_out])
    mine = lax.ppermute(both, EVERY, exchange_pairs(0))
    far = lax.ppermute(both, EVERY, exchange_pairs(1))
    low = lax.axis_index("h") == 0
    out = []
    for s in range(2):
        pair = jnp.stack([jnp.where(low, mine[s], far[s]), jnp.where(low, far[s], mine[s])])
        pair = jnp.broadcast_to(pair[None], (nz,) + pair.shape)
        out.append(swap_all_to_all(after(pair, out[0]) if out else pair, "z"))
    return out


def gather_core(one):
    t, d = one.shape[-2:]
    ny = SIZES["y"]
    first = lax.axis_index("c") == 0
    other = other_core(one)
    part = jnp.stack([jnp.where(first, one, other), jnp.where(first, other, one)], axis=2)
    return part.reshape(ny, -1, t, d).transpose(0, 2, 1, 3).reshape(ny * t, -1)


def after(value, others):
    return value if others is None else lax.optimization_barrier((value, others))[0]


def trade(blocks, axis, partners):
    return [lax.ppermute(b, axis, p) for b, p in zip(blocks, partners)]


def xor_trade(value, step):
    return lax.ppermute(value, "y", [(i, i ^ step) for i in range(SIZES["y"])])


def scatter_grad_tokens(pieces):
    low = lax.axis_index("h") == 0
    pieces = sum_first(swap_all_to_all(pieces, "z"))
    near = jnp.where(low, pieces[0], pieces[1])
    far = jnp.where(low, pieces[1], pieces[0])
    sums = near
    near = lax.ppermute(near, EVERY, exchange_pairs(0, True))
    far = lax.ppermute(far, EVERY, exchange_pairs(1, True))
    return (near + far).astype(BF), sums


def body(tokens, grad_out, w_gate, w_up, w_down):
    nx, ny = SIZES["x"], SIZES["y"]
    rows = w_gate.shape[0]
    t, d = tokens.shape
    x_partners = [[(i, (i + k) % nx) for i in range(nx)] for k in (1, nx - 1, 2)]
    w_down_t = w_down.T
    weights = []
    at = 0
    for width in WIDTHS:
        part = slice(at, at + width)
        at += width
        own = jnp.concatenate([w_gate[:, part], w_up[:, part], w_down_t[:, part]], axis=1)
        weights.append(lax.all_gather(own, "x", axis=0, tiled=True))
    one_x, one_dy = gather_tokens(tokens, grad_out)
    x2, dy2 = gather_core(one_x), None
    rotor = hadamard(HB)
    me = lax.axis_index("x")

    half = 2 * t
    kept, fulls = [], []
    done = None
    for w, width in zip(weights, WIDTHS):
        w = after(w, done)
        cut = 2 * width
        give = [dot(x2[half:], w[:, :cut], ((1,), (0,))).astype(BF)]
        if dy2 is None:
            dy2 = gather_core(after(one_dy, give))
        give.append(dot(dy2[half:], w[:, cut:], ((1,), (0,))).astype(BF))
        sides = [(x2, w[:, :cut]), (dy2, w[:, cut:])]
        if kept:
            got = [xor_trade(jnp.concatenate(give, axis=1), 1)]
            got = [got[0][:, :cut], got[0][:, cut:]]
        else:
            got = [xor_trade(g, 1) for g in give]
        keep = [dot(v[:half], u, ((1,), (0,))) for v, u in sides]
        keep = [k + g.astype(F32) for k, g in zip(keep, got)]
        done = jnp.concatenate([k[t:].astype(BF) for k in keep], axis=1)
        kept.append(([k[:t] for k in keep], xor_trade(done, 2)))

    for ((gu, d_hidden), got), width in zip(kept, WIDTHS):
        gu = gu + got[:, : 2 * width].astype(F32)
        d_hidden = d_hidden + got[:, 2 * width :].astype(F32)
        gate, up = gu[:, :width], gu[:, width:]
        sig = jax.nn.sigmoid(gate)
        active = gate * sig
        hidden = (active * up).astype(BF)
        d_gate = (d_hidden * up * sig * (1.0 + gate * (1.0 - sig))).astype(BF)
        d_up = (d_hidden * active).astype(BF)
        mine = jnp.concatenate([d_gate, d_up, hidden], axis=1)
        mine = jnp.concatenate([mine, xor_trade(mine, 2)], axis=0)
        fulls.append(jnp.concatenate([mine, xor_trade(mine, 1)], axis=0))

    def columns(v, step):
        return lax.dynamic_slice_in_dim(v, lax.rem(me + step, nx) * rows, rows, axis=1)

    steps = (0, 1, nx - 1, 2)
    x_cols = [columns(x2, s) for s in steps]
    dy_cols = [columns(dy2, s) for s in steps]

    first = lax.axis_index("c") == 0

    def core_rows(w, own):
        w = w.reshape(-1, 2, d, w.shape[1])
        return jnp.where(first == own, w[:, 0], w[:, 1]).reshape(-1, w.shape[-1])

    sums = []
    give = keep = 0.0
    done = None
    for full, w, width in zip(fulls, weights, WIDTHS):
        full = after(full, done)
        dgu, hid = full[:, : 2 * width], full[:, 2 * width :]
        give = give + dot(dgu, core_rows(w[:, : 2 * width], False), ((1,), (1,)))
        if len(sums) == len(WIDTHS) - 1:
            dgu, hid = after((dgu, hid), give)

        def piece(k):
            return jnp.concatenate(
                [dot(x_cols[k], dgu, ((0,), (0,))), dot(dy_cols[k], hid, ((0,), (0,)))], axis=1
            )

        send = [piece(k).astype(BF) for k in range(1, nx)]
        got = trade(send, "x", x_partners)
        done = got[0]
        keep = keep + dot(dgu, core_rows(w[:, : 2 * width], True), ((1,), (1,)))
        sums.append((piece(0), got))
    pieces = (keep + other_core(give)).astype(BF).reshape(ny, t, -1, d)
    pieces = pieces.transpose(0, 2, 1, 3).reshape(SIZES["z"], -1, t, d)
    grad_tokens, late = scatter_grad_tokens(pieces)

    gates, ups, downs = [], [], []
    for (gw, got), width in zip(sums, WIDTHS):
        gw = after(gw, late if got[0] is done else pieces)
        for g in got:
            gw = gw + g.astype(F32)
        gw = gw.reshape(rows // HB, HB, 3 * width)
        rot = jnp.einsum(
            "ij,bjf->bif", rotor, gw[:, :, : 2 * width], precision=lax.Precision.HIGHEST
        ).astype(BF)
        rot = rot.reshape(rows, 2 * width)
        gates.append(rot[:, :width])
        ups.append(rot[:, width:])
        downs.append(
            jnp.einsum(
                "bjf,ij->fbi", gw[:, :, 2 * width :], rotor, precision=lax.Precision.HIGHEST
            )
            .reshape(width, rows)
            .astype(BF)
        )
    return (
        grad_tokens,
        jnp.concatenate(gates, axis=1),
        jnp.concatenate(ups, axis=1),
        jnp.concatenate(downs, axis=0),
    )


def solution(mesh):
    fine = Mesh(mesh.devices.reshape(tuple(SIZES[a] for a in EVERY)), EVERY)
    return jax.shard_map(
        body,
        mesh=fine,
        in_specs=(P(FSDP, REP), P(FSDP, REP), P(FSDP, REP), P(FSDP, REP), P(REP, FSDP)),
        out_specs=(P(FSDP, REP), P(FSDP, REP), P(FSDP, REP), P(REP, FSDP)),
        check_vma=False,
    )
```

```python
import math

import jax
import jax.numpy as jnp
from jax import lax
from jax.sharding import Mesh
from jax.sharding import PartitionSpec as P

HB = 128
WIDTHS = (384, 384)
SIZES = {"z": 8, "h": 2, "c": 2, "y": 4, "x": 4}
EVERY = ("z", "h", "c", "y", "x")
REP = ("z", "h", "c")
FSDP = ("y", "x")
BF = jnp.bfloat16
F32 = jnp.float32


def hadamard(size):
    index = jnp.arange(size, dtype=jnp.int32)
    both = index[:, None] & index[None, :]
    parity = jnp.zeros((size, size), jnp.int32)
    for bit_pos in range(size.bit_length() - 1):
        parity = parity + (both >> bit_pos & 1)
    return (1 - 2 * (parity % 2)).astype(F32) / math.sqrt(size)


ORDER = (0, 2, 1, 3)


def exchange_pairs(flip, back=False):
    nz, nh, nc, ny, nx = (SIZES[a] for a in EVERY)
    pairs = []
    for z in range(nz):
        for h in range(nh):
            for c in range(nc):
                for y in range(ny):
                    for x in range(nx):
                        src = (((z * nh + h) * nc + c) * ny + y) * nx + x
                        yy, hh = z // 2, h ^ flip
                        zz = 2 * ORDER[y ^ yy] + z % 2
                        dst = (((zz * nh + hh) * nc + c) * ny + yy) * nx + x
                        pairs.append((dst, src) if back else (src, dst))
    return pairs


def dot(left, right, dims):
    return lax.dot_general(left, right, (dims, ((), ())), preferred_element_type=F32)


def swap_all_to_all(value, axes):
    return lax.all_to_all(value, axes, split_axis=0, concat_axis=0, tiled=True)


def sum_first(value):
    terms = [value[i].astype(F32) for i in range(value.shape[0])]
    while len(terms) > 1:
        terms = [a + b for a, b in zip(terms[::2], terms[1::2])]
    return terms[0]


def other_core(value):
    return lax.ppermute(value, "c", [(0, 1), (1, 0)])


def gather_tokens(tokens, grad_out):
    nz, ny = SIZES["z"], SIZES["y"]
    t, d = tokens.shape
    both = jnp.stack([tokens, grad_out])
    mine = lax.ppermute(both, EVERY, exchange_pairs(0))
    far = lax.ppermute(both, EVERY, exchange_pairs(1))
    low = lax.axis_index("h") == 0
    pair = jnp.stack([jnp.where(low, mine, far), jnp.where(low, far, mine)])
    one = swap_all_to_all(jnp.broadcast_to(pair[None], (nz,) + pair.shape), "z")
    one = one.reshape(ny, -1, 2, t, d).transpose(2, 0, 3, 1, 4).reshape(2, ny * t, -1)
    return one, other_core(one)


def after(value, others):
    return value if others is None else lax.optimization_barrier((value, others))[0]


def trade(blocks, axis, partners):
    return [lax.ppermute(b, axis, p) for b, p in zip(blocks, partners)]


def xor_trade(value, step):
    return lax.ppermute(value, "y", [(i, i ^ step) for i in range(SIZES["y"])])


def scatter_grad_tokens(pieces):
    low = lax.axis_index("h") == 0
    pieces = sum_first(swap_all_to_all(pieces, "z"))
    near = jnp.where(low, pieces[0], pieces[1])
    far = jnp.where(low, pieces[1], pieces[0])
    sums = near
    near = lax.ppermute(near, EVERY, exchange_pairs(0, True))
    far = lax.ppermute(far, EVERY, exchange_pairs(1, True))
    return (near + far).astype(BF), sums


def body(tokens, grad_out, w_gate, w_up, w_down):
    nx, ny = SIZES["x"], SIZES["y"]
    rows = w_gate.shape[0]
    t, d = tokens.shape
    x_partners = [[(i, (i + k) % nx) for i in range(nx)] for k in (1, nx - 1, 2)]
    first = lax.axis_index("c") == 0
    n = rows // 2

    def own_first(w):
        return jnp.where(first, w, jnp.concatenate([w[n:], w[:n]], axis=0)).reshape(2, n, -1)

    parts = [own_first(w) for w in (w_gate, w_up, w_down.T)]
    weights = []
    at = 0
    for width in WIDTHS:
        own = [p[c, :, at : at + width] for c in range(2) for p in parts]
        at += width
        w = lax.all_gather(jnp.concatenate(own, axis=1), "x", axis=0, tiled=True)
        weights.append(w)
    near, far = gather_tokens(tokens, grad_out)
    rotor = hadamard(HB)
    me = lax.axis_index("x")

    half = 2 * t
    kept, fulls = [], []
    done = None
    for w, width in zip(weights, WIDTHS):
        w = after(w, done)
        cut = 2 * width
        spans = [(0, 0, cut), (1, cut, 3 * width)]

        def share(part):
            return [
                dot(near[s, part], w[:, lo:hi], ((1,), (0,)))
                + dot(far[s, part], w[:, 3 * width + lo : 3 * width + hi], ((1,), (0,)))
                for s, lo, hi in spans
            ]

        give = [g.astype(BF) for g in share(slice(half, None))]
        got = xor_trade(jnp.concatenate(give, axis=1), 1)
        got = [got[:, :cut], got[:, cut:]]
        keep = [k + g.astype(F32) for k, g in zip(share(slice(0, half)), got)]
        done = jnp.concatenate([k[t:].astype(BF) for k in keep], axis=1)
        kept.append(([k[:t] for k in keep], xor_trade(done, 2)))

    for ((gu, d_hidden), got), width in zip(kept, WIDTHS):
        gu = gu + got[:, : 2 * width].astype(F32)
        d_hidden = d_hidden + got[:, 2 * width :].astype(F32)
        gate, up = gu[:, :width], gu[:, width:]
        sig = jax.nn.sigmoid(gate)
        active = gate * sig
        hidden = (active * up).astype(BF)
        d_gate = (d_hidden * up * sig * (1.0 + gate * (1.0 - sig))).astype(BF)
        d_up = (d_hidden * active).astype(BF)
        mine = jnp.concatenate([d_gate, d_up, hidden], axis=1)
        mine = jnp.concatenate([mine, xor_trade(mine, 2)], axis=0)
        fulls.append(jnp.concatenate([mine, xor_trade(mine, 1)], axis=0))

    def columns(s, step):
        v = jnp.stack([near[s].reshape(ny * t, nx, n), far[s].reshape(ny * t, nx, n)], axis=2)
        v = v.reshape(ny * t, nx * rows)
        return lax.dynamic_slice_in_dim(v, lax.rem(me + step, nx) * rows, rows, axis=1)

    steps = (0, 1, nx - 1, 2)
    x_cols = [columns(0, s) for s in steps]
    dy_cols = [columns(1, s) for s in steps]

    sums = []
    give = keep = 0.0
    done = None
    for full, w, width in zip(fulls, weights, WIDTHS):
        last = len(sums) == len(WIDTHS) - 1
        full = after(full, done)
        dgu, hid = full[:, : 2 * width], full[:, 2 * width :]
        give = give + dot(dgu, w[:, 3 * width : 5 * width], ((1,), (1,)))
        if last:
            dgu, hid = after((dgu, hid), give)

        def piece(k):
            return jnp.concatenate(
                [dot(x_cols[k], dgu, ((0,), (0,))), dot(dy_cols[k], hid, ((0,), (0,)))], axis=1
            )

        send = [piece(k).astype(BF) for k in range(1, nx)]
        got = trade(send[:2], "x", x_partners)
        done = got
        got = got + trade([send[2] if last else after(send[2], got)], "x", x_partners[2:])
        keep = keep + dot(dgu, w[:, : 2 * width], ((1,), (1,)))
        sums.append((piece(0), got))
    pieces = (keep + other_core(give)).astype(BF).reshape(ny, t, -1, d)
    pieces = pieces.transpose(0, 2, 1, 3).reshape(SIZES["z"], -1, t, d)
    grad_tokens, late = scatter_grad_tokens(pieces)

    gates, ups, downs = [], [], []
    for (gw, got), width in zip(sums, WIDTHS):
        gw = after(gw, late if got is sums[-1][1] else pieces)
        for g in got:
            gw = gw + g.astype(F32)
        gw = jnp.where(first, gw, jnp.concatenate([gw[n:], gw[:n]], axis=0))
        gw = gw.reshape(rows // HB, HB, 3 * width)
        rot = jnp.einsum(
            "ij,bjf->bif", rotor, gw[:, :, : 2 * width], precision=lax.Precision.HIGHEST
        ).astype(BF)
        rot = rot.reshape(rows, 2 * width)
        gates.append(rot[:, :width])
        ups.append(rot[:, width:])
        downs.append(
            jnp.einsum(
                "bjf,ij->fbi", gw[:, :, 2 * width :], rotor, precision=lax.Precision.HIGHEST
            )
            .reshape(width, rows)
            .astype(BF)
        )
    return (
        grad_tokens,
        jnp.concatenate(gates, axis=1),
        jnp.concatenate(ups, axis=1),
        jnp.concatenate(downs, axis=0),
    )


def solution(mesh):
    fine = Mesh(mesh.devices.reshape(tuple(SIZES[a] for a in EVERY)), EVERY)
    return jax.shard_map(
        body,
        mesh=fine,
        in_specs=(P(FSDP, REP), P(FSDP, REP), P(FSDP, REP), P(FSDP, REP), P(REP, FSDP)),
        out_specs=(P(FSDP, REP), P(FSDP, REP), P(FSDP, REP), P(REP, FSDP)),
        check_vma=False,
    )
```

```python
import math

import jax
import jax.numpy as jnp
from jax import lax
from jax.sharding import Mesh
from jax.sharding import PartitionSpec as P

HB = 128
WIDTHS = (384, 384)
SIZES = {"z": 8, "h": 2, "c": 2, "y": 4, "x": 4}
EVERY = ("z", "h", "c", "y", "x")
REP = ("z", "h", "c")
FSDP = ("y", "x")
BF = jnp.bfloat16
F32 = jnp.float32


def hadamard(size):
    index = jnp.arange(size, dtype=jnp.int32)
    both = index[:, None] & index[None, :]
    parity = jnp.zeros((size, size), jnp.int32)
    for bit_pos in range(size.bit_length() - 1):
        parity = parity + (both >> bit_pos & 1)
    return (1 - 2 * (parity % 2)).astype(F32) / math.sqrt(size)


ORDER = (0, 2, 1, 3)


def exchange_pairs(flip, back=False):
    nz, nh, nc, ny, nx = (SIZES[a] for a in EVERY)
    pairs = []
    for z in range(nz):
        for h in range(nh):
            for c in range(nc):
                for y in range(ny):
                    for x in range(nx):
                        src = (((z * nh + h) * nc + c) * ny + y) * nx + x
                        yy, hh = z // 2, h ^ flip
                        zz = 2 * ORDER[y ^ yy] + z % 2
                        dst = (((zz * nh + hh) * nc + c) * ny + yy) * nx + x
                        pairs.append((dst, src) if back else (src, dst))
    return pairs


def dot(left, right, dims):
    return lax.dot_general(left, right, (dims, ((), ())), preferred_element_type=F32)


def swap_all_to_all(value, axes):
    return lax.all_to_all(value, axes, split_axis=0, concat_axis=0, tiled=True)


def sum_first(value):
    terms = [value[i].astype(F32) for i in range(value.shape[0])]
    while len(terms) > 1:
        terms = [a + b for a, b in zip(terms[::2], terms[1::2])]
    return terms[0]


def other_core(value):
    return lax.ppermute(value, "c", [(0, 1), (1, 0)])


def gather_tokens(tokens, grad_out):
    nz, ny = SIZES["z"], SIZES["y"]
    t, d = tokens.shape
    both = jnp.stack([tokens, grad_out])
    mine = lax.ppermute(both, EVERY, exchange_pairs(0))
    far = lax.ppermute(both, EVERY, exchange_pairs(1))
    low = lax.axis_index("h") == 0
    first = lax.axis_index("c") == 0
    out = []
    for s in range(2):
        pair = jnp.stack([jnp.where(low, mine[s], far[s]), jnp.where(low, far[s], mine[s])])
        pair = jnp.broadcast_to(pair[None], (nz,) + pair.shape)
        if out:
            pair = after(pair, one)
        one = swap_all_to_all(pair, "z")
        other = other_core(one)
        part = jnp.stack([jnp.where(first, one, other), jnp.where(first, other, one)], axis=2)
        out.append(part.reshape(ny, -1, t, d).transpose(0, 2, 1, 3).reshape(ny * t, -1))
    return out


def after(value, others):
    return value if others is None else lax.optimization_barrier((value, others))[0]


def trade(blocks, axis, partners):
    return [lax.ppermute(b, axis, p) for b, p in zip(blocks, partners)]


def xor_trade(value, step):
    return lax.ppermute(value, "y", [(i, i ^ step) for i in range(SIZES["y"])])


def scatter_grad_tokens(pieces):
    pieces = swap_all_to_all(pieces, ("z", "h"))
    return lax.ppermute(sum_first(pieces).astype(BF), EVERY, exchange_pairs(0, True))


def body(tokens, grad_out, w_gate, w_up, w_down):
    nx, ny = SIZES["x"], SIZES["y"]
    rows = w_gate.shape[0]
    t, d = tokens.shape
    x_partners = [[(i, (i + k) % nx) for i in range(nx)] for k in (1, nx - 1, 2)]
    w_down_t = w_down.T
    weights = []
    at = 0
    for width in WIDTHS:
        part = slice(at, at + width)
        at += width
        own = jnp.concatenate([w_gate[:, part], w_up[:, part], w_down_t[:, part]], axis=1)
        weights.append(lax.all_gather(own, "x", axis=0, tiled=True))
    x2, dy2 = gather_tokens(tokens, grad_out)
    rotor = hadamard(HB)
    me = lax.axis_index("x")

    half = 2 * t
    kept, fulls = [], []
    done = None
    for w, width in zip(weights, WIDTHS):
        w = after(w, done)
        cut = 2 * width
        sides = [(x2, w[:, :cut]), (dy2, w[:, cut:])]
        give = [dot(v[half:], u, ((1,), (0,))).astype(BF) for v, u in sides]
        if kept:
            got = [xor_trade(jnp.concatenate(give, axis=1), 1)]
            got = [got[0][:, :cut], got[0][:, cut:]]
        else:
            got = [xor_trade(g, 1) for g in give]
        keep = [dot(v[:half], u, ((1,), (0,))) for v, u in sides]
        keep = [k + g.astype(F32) for k, g in zip(keep, got)]
        done = jnp.concatenate([k.astype(BF) for k in keep], axis=1)
        done = jnp.concatenate([done[t:], done[:t]], axis=0)
        kept.append((keep, xor_trade(done, 2)))

    for ((gu, d_hidden), got), width in zip(kept, WIDTHS):
        gu = gu + got[:, : 2 * width].astype(F32)
        d_hidden = d_hidden + got[:, 2 * width :].astype(F32)
        gate, up = gu[:, :width], gu[:, width:]
        sig = jax.nn.sigmoid(gate)
        active = gate * sig
        hidden = (active * up).astype(BF)
        d_gate = (d_hidden * up * sig * (1.0 + gate * (1.0 - sig))).astype(BF)
        d_up = (d_hidden * active).astype(BF)
        mine = jnp.concatenate([d_gate, d_up, hidden], axis=1)
        fulls.append(jnp.concatenate([mine, xor_trade(mine, 1)], axis=0))

    def columns(v, step):
        return lax.dynamic_slice_in_dim(v, lax.rem(me + step, nx) * rows, rows, axis=1)

    steps = (0, 1, nx - 1, 2)
    x_cols = [columns(x2, s) for s in steps]
    dy_cols = [columns(dy2, s) for s in steps]

    first = lax.axis_index("c") == 0

    def core_rows(w, own):
        w = w.reshape(-1, 2, d, w.shape[1])
        return jnp.where(first == own, w[:, 0], w[:, 1]).reshape(-1, w.shape[-1])

    sums = []
    give = keep = 0.0
    done = None
    for full, w, width in zip(fulls, weights, WIDTHS):
        full = after(full, done)
        dgu, hid = full[:, : 2 * width], full[:, 2 * width :]
        give = give + dot(dgu, core_rows(w[:, : 2 * width], False), ((1,), (1,)))
        if len(sums) == len(WIDTHS) - 1:
            dgu, hid = after((dgu, hid), give)

        def piece(k):
            return jnp.concatenate(
                [dot(x_cols[k], dgu, ((0,), (0,))), dot(dy_cols[k], hid, ((0,), (0,)))], axis=1
            )

        send = [piece(k).astype(BF) for k in range(1, nx)]
        got = trade(send, "x", x_partners)
        done = got[0]
        keep = keep + dot(dgu, core_rows(w[:, : 2 * width], True), ((1,), (1,)))
        sums.append((piece(0), got))
    pieces = (keep + other_core(give)).astype(BF).reshape(ny, t, -1, d)
    pieces = pieces.transpose(0, 2, 1, 3).reshape(-1, t, d)
    grad_tokens = scatter_grad_tokens(pieces)

    gates, ups, downs = [], [], []
    for (gw, got), width in zip(sums, WIDTHS):
        gw = after(gw, pieces)
        for g in got:
            gw = gw + g.astype(F32)
        gw = gw.reshape(rows // HB, HB, 3 * width)
        rot = jnp.einsum(
            "ij,bjf->bif", rotor, gw[:, :, : 2 * width], precision=lax.Precision.HIGHEST
        ).astype(BF)
        rot = rot.reshape(rows, 2 * width)
        gates.append(rot[:, :width])
        ups.append(rot[:, width:])
        downs.append(
            jnp.einsum(
                "bjf,ij->fbi", gw[:, :, 2 * width :], rotor, precision=lax.Precision.HIGHEST
            )
            .reshape(width, rows)
            .astype(BF)
        )
    return (
        grad_tokens,
        jnp.concatenate(gates, axis=1),
        jnp.concatenate(ups, axis=1),
        jnp.concatenate(downs, axis=0),
    )


def solution(mesh):
    fine = Mesh(mesh.devices.reshape(tuple(SIZES[a] for a in EVERY)), EVERY)
    return jax.shard_map(
        body,
        mesh=fine,
        in_specs=(P(FSDP, REP), P(FSDP, REP), P(FSDP, REP), P(FSDP, REP), P(REP, FSDP)),
        out_specs=(P(FSDP, REP), P(FSDP, REP), P(FSDP, REP), P(REP, FSDP)),
        check_vma=False,
    )
```

```python
import math

import jax
import jax.numpy as jnp
from jax import lax
from jax.experimental import pallas as pl
from jax.experimental.pallas import tpu as pltpu
from jax.sharding import Mesh
from jax.sharding import PartitionSpec as P

HB = 128
WIDTHS = (384, 384)
SIZES = {"z": 8, "h": 2, "c": 2, "y": 4, "x": 4}
EVERY = ("z", "h", "c", "y", "x")
REP = ("z", "h", "c")
FSDP = ("y", "x")
BF = jnp.bfloat16
F32 = jnp.float32


def hadamard(size):
    index = jnp.arange(size, dtype=jnp.int32)
    both = index[:, None] & index[None, :]
    parity = jnp.zeros((size, size), jnp.int32)
    for bit_pos in range(size.bit_length() - 1):
        parity = parity + (both >> bit_pos & 1)
    return (1 - 2 * (parity % 2)).astype(F32) / math.sqrt(size)


ORDER = (0, 2, 1, 3)


def exchange_pairs(flip, back=False):
    nz, nh, nc, ny, nx = (SIZES[a] for a in EVERY)
    pairs = []
    for z in range(nz):
        for h in range(nh):
            for c in range(nc):
                for y in range(ny):
                    for x in range(nx):
                        src = (((z * nh + h) * nc + c) * ny + y) * nx + x
                        yy, hh = z // 2, h ^ flip
                        zz = 2 * ORDER[y ^ yy] + z % 2
                        dst = (((zz * nh + hh) * nc + c) * ny + yy) * nx + x
                        pairs.append((dst, src) if back else (src, dst))
    return pairs


def dot(left, right, dims):
    return lax.dot_general(left, right, (dims, ((), ())), preferred_element_type=F32)


def swap_all_to_all(value, axes):
    return lax.all_to_all(value, axes, split_axis=0, concat_axis=0, tiled=True)


def sum_first(value):
    terms = [value[i].astype(F32) for i in range(value.shape[0])]
    while len(terms) > 1:
        terms = [a + b for a, b in zip(terms[::2], terms[1::2])]
    return terms[0]


def other_core(value):
    return lax.ppermute(value, "c", [(0, 1), (1, 0)])


def place_blocks(core, mine, theirs, x_out, dy_out):
    t, d = mine.shape[-2:]
    for source, c in ((mine, core[0]), (theirs, 1 - core[0])):
        for z in range(mine.shape[0]):
            for h in range(2):
                at = pl.ds(pl.multiple_of((((z % 2) * 2 + h) * 2 + c) * d, d), d)
                for s, out in enumerate((x_out, dy_out)):
                    out[pl.ds(z // 2 * t, t), at] = source[z, h, s]


def gather_tokens(tokens, grad_out):
    nz, ny = SIZES["z"], SIZES["y"]
    t, d = tokens.shape
    both = jnp.stack([tokens, grad_out])
    mine = lax.ppermute(both, EVERY, exchange_pairs(0))
    far = lax.ppermute(both, EVERY, exchange_pairs(1))
    low = lax.axis_index("h") == 0
    pair = jnp.stack([jnp.where(low, mine, far), jnp.where(low, far, mine)])
    one = swap_all_to_all(jnp.broadcast_to(pair[None], (nz,) + pair.shape), "z")
    shape = jax.ShapeDtypeStruct((ny * t, d * nz), BF)
    vmem = pl.BlockSpec(memory_space=pltpu.VMEM)
    return pl.pallas_call(
        place_blocks,
        out_shape=(shape, shape),
        in_specs=[pl.BlockSpec(memory_space=pltpu.SMEM), vmem, vmem],
        out_specs=(vmem, vmem),
        compiler_params=pltpu.CompilerParams(vmem_limit_bytes=16 * 2**20),
        cost_estimate=pl.CostEstimate(flops=0, bytes_accessed=2**22, transcendentals=0),
    )(lax.axis_index("c").astype(jnp.int32)[None], one, other_core(one))


def after(value, others):
    return value if others is None else lax.optimization_barrier((value, others))[0]


def trade(blocks, axis, partners):
    return [lax.ppermute(b, axis, p) for b, p in zip(blocks, partners)]


def xor_trade(value, step):
    return lax.ppermute(value, "y", [(i, i ^ step) for i in range(SIZES["y"])])


def scatter_grad_tokens(pieces):
    pieces = swap_all_to_all(pieces, ("z", "h"))
    return lax.ppermute(sum_first(pieces).astype(BF), EVERY, exchange_pairs(0, True))


def body(tokens, grad_out, w_gate, w_up, w_down):
    nx, ny = SIZES["x"], SIZES["y"]
    rows = w_gate.shape[0]
    t, d = tokens.shape
    x_partners = [[(i, (i + k) % nx) for i in range(nx)] for k in (1, nx - 1, 2)]
    w_down_t = w_down.T
    weights = []
    at = 0
    for width in WIDTHS:
        part = slice(at, at + width)
        at += width
        own = jnp.concatenate([w_gate[:, part], w_up[:, part], w_down_t[:, part]], axis=1)
        weights.append(lax.all_gather(own, "x", axis=0, tiled=True))
    x2, dy2 = gather_tokens(tokens, grad_out)
    rotor = hadamard(HB)
    me = lax.axis_index("x")

    half = 2 * t
    kept, fulls = [], []
    done = None
    for w, width in zip(weights, WIDTHS):
        w = after(w, done)
        cut = 2 * width
        sides = [(x2, w[:, :cut]), (dy2, w[:, cut:])]
        give = [dot(v[half:], u, ((1,), (0,))).astype(BF) for v, u in sides]
        got = xor_trade(jnp.concatenate(give, axis=1), 1)
        got = [got[:, :cut], got[:, cut:]]
        keep = [dot(v[:half], u, ((1,), (0,))) for v, u in sides]
        keep = [k + g.astype(F32) for k, g in zip(keep, got)]
        done = jnp.concatenate([k.astype(BF) for k in keep], axis=1)
        done = jnp.concatenate([done[t:], done[:t]], axis=0)
        kept.append((keep, xor_trade(done, 2)))

    for ((gu, d_hidden), got), width in zip(kept, WIDTHS):
        gu = gu + got[:, : 2 * width].astype(F32)
        d_hidden = d_hidden + got[:, 2 * width :].astype(F32)
        gate, up = gu[:, :width], gu[:, width:]
        sig = jax.nn.sigmoid(gate)
        active = gate * sig
        hidden = (active * up).astype(BF)
        d_gate = (d_hidden * up * sig * (1.0 + gate * (1.0 - sig))).astype(BF)
        d_up = (d_hidden * active).astype(BF)
        mine = jnp.concatenate([d_gate, d_up, hidden], axis=1)
        fulls.append(jnp.concatenate([mine, xor_trade(mine, 1)], axis=0))

    def columns(v, step):
        return lax.dynamic_slice_in_dim(v, lax.rem(me + step, nx) * rows, rows, axis=1)

    steps = (0, 1, nx - 1, 2)
    x_cols = [columns(x2, s) for s in steps]
    dy_cols = [columns(dy2, s) for s in steps]

    first = lax.axis_index("c") == 0

    def core_rows(w, own):
        w = w.reshape(-1, 2, d, w.shape[1])
        return jnp.where(first == own, w[:, 0], w[:, 1]).reshape(-1, w.shape[-1])

    sums = []
    give = keep = 0.0
    done = None
    for full, w, width in zip(fulls, weights, WIDTHS):
        full = after(full, done)
        dgu, hid = full[:, : 2 * width], full[:, 2 * width :]
        give = give + dot(dgu, core_rows(w[:, : 2 * width], False), ((1,), (1,)))
        last = len(sums) == len(WIDTHS) - 1
        if last:
            dgu, hid = after((dgu, hid), give)

        def piece(k):
            return jnp.concatenate(
                [dot(x_cols[k], dgu, ((0,), (0,))), dot(dy_cols[k], hid, ((0,), (0,)))], axis=1
            )

        send = [piece(k).astype(BF) for k in range(1, nx)]
        got = trade(send[:1], "x", x_partners)
        done = got
        keep = keep + dot(dgu, core_rows(w[:, : 2 * width], True), ((1,), (1,)))
        rest = send[1:]
        if last:
            pieces = (keep + other_core(give)).astype(BF).reshape(ny, t, -1, d)
            pieces = pieces.transpose(0, 2, 1, 3).reshape(-1, t, d)
            rest = after(rest, pieces)
        got = got + trade(rest, "x", x_partners[1:])
        sums.append((piece(0), got))
    grad_tokens = scatter_grad_tokens(pieces)

    gates, ups, downs = [], [], []
    for (gw, got), width in zip(sums, WIDTHS):
        gw = after(gw, (pieces, gates, ups, downs))
        for g in got:
            gw = gw + g.astype(F32)
        gw = gw.reshape(rows // HB, HB, 3 * width)
        rot = jnp.einsum(
            "ij,bjf->bif", rotor, gw[:, :, : 2 * width], precision=lax.Precision.HIGHEST
        ).astype(BF)
        rot = rot.reshape(rows, 2 * width)
        gates.append(rot[:, :width])
        ups.append(rot[:, width:])
        downs.append(
            jnp.einsum(
                "bjf,ij->fbi", gw[:, :, 2 * width :], rotor, precision=lax.Precision.HIGHEST
            )
            .reshape(width, rows)
            .astype(BF)
        )
    return (
        grad_tokens,
        jnp.concatenate(gates, axis=1),
        jnp.concatenate(ups, axis=1),
        jnp.concatenate(downs, axis=0),
    )


def solution(mesh):
    fine = Mesh(mesh.devices.reshape(tuple(SIZES[a] for a in EVERY)), EVERY)
    return jax.shard_map(
        body,
        mesh=fine,
        in_specs=(P(FSDP, REP), P(FSDP, REP), P(FSDP, REP), P(FSDP, REP), P(REP, FSDP)),
        out_specs=(P(FSDP, REP), P(FSDP, REP), P(FSDP, REP), P(REP, FSDP)),
        check_vma=False,
    )
```

```python
import math

import jax
import jax.numpy as jnp
from jax import lax
from jax.experimental import pallas as pl
from jax.experimental.pallas import tpu as pltpu
from jax.sharding import Mesh
from jax.sharding import PartitionSpec as P

HB = 128
WIDTHS = (384, 384)
SIZES = {"z": 8, "h": 2, "c": 2, "y": 4, "x": 4}
EVERY = ("z", "h", "c", "y", "x")
REP = ("z", "h", "c")
FSDP = ("y", "x")
BF = jnp.bfloat16
F32 = jnp.float32


def hadamard(size):
    index = jnp.arange(size, dtype=jnp.int32)
    both = index[:, None] & index[None, :]
    parity = jnp.zeros((size, size), jnp.int32)
    for bit_pos in range(size.bit_length() - 1):
        parity = parity + (both >> bit_pos & 1)
    return (1 - 2 * (parity % 2)).astype(F32) / math.sqrt(size)


ORDER = (0, 2, 1, 3)


def exchange_pairs(flip, back=False):
    nz, nh, nc, ny, nx = (SIZES[a] for a in EVERY)
    pairs = []
    for z in range(nz):
        for h in range(nh):
            for c in range(nc):
                for y in range(ny):
                    for x in range(nx):
                        src = (((z * nh + h) * nc + c) * ny + y) * nx + x
                        yy, hh = z // 2, h ^ flip
                        zz = 2 * ORDER[y ^ yy] + z % 2
                        dst = (((zz * nh + hh) * nc + c) * ny + yy) * nx + x
                        pairs.append((dst, src) if back else (src, dst))
    return pairs


def dot(left, right, dims):
    return lax.dot_general(left, right, (dims, ((), ())), preferred_element_type=F32)


def swap_all_to_all(value, axes):
    return lax.all_to_all(value, axes, split_axis=0, concat_axis=0, tiled=True)


def sum_first(value):
    terms = [value[i].astype(F32) for i in range(value.shape[0])]
    while len(terms) > 1:
        terms = [a + b for a, b in zip(terms[::2], terms[1::2])]
    return terms[0]


def other_core(value):
    return lax.ppermute(value, "c", [(0, 1), (1, 0)])


def place_blocks(core, mine, theirs, x_out, dy_out):
    t, d = mine.shape[-2:]
    for source, c in ((mine, core[0]), (theirs, 1 - core[0])):
        for z in range(mine.shape[0]):
            for h in range(2):
                at = pl.ds(pl.multiple_of((((z % 2) * 2 + h) * 2 + c) * d, d), d)
                for s, out in enumerate((x_out, dy_out)):
                    out[pl.ds(z // 2 * t, t), at] = source[z, h, s]


def gather_tokens(tokens, grad_out):
    nz, ny = SIZES["z"], SIZES["y"]
    t, d = tokens.shape
    both = jnp.stack([tokens, grad_out])
    mine = lax.ppermute(both, EVERY, exchange_pairs(0))
    far = lax.ppermute(both, EVERY, exchange_pairs(1))
    low = lax.axis_index("h") == 0
    pair = jnp.stack([jnp.where(low, mine, far), jnp.where(low, far, mine)])
    one = swap_all_to_all(jnp.broadcast_to(pair[None], (nz,) + pair.shape), "z")
    shape = jax.ShapeDtypeStruct((ny * t, d * nz), BF)
    vmem = pl.BlockSpec(memory_space=pltpu.VMEM)
    return pl.pallas_call(
        place_blocks,
        out_shape=(shape, shape),
        in_specs=[pl.BlockSpec(memory_space=pltpu.SMEM), vmem, vmem],
        out_specs=(vmem, vmem),
        compiler_params=pltpu.CompilerParams(vmem_limit_bytes=16 * 2**20),
        cost_estimate=pl.CostEstimate(flops=0, bytes_accessed=2**22, transcendentals=0),
    )(lax.axis_index("c").astype(jnp.int32)[None], one, other_core(one))


def after(value, others):
    return value if others is None else lax.optimization_barrier((value, others))[0]


def trade(blocks, axis, partners):
    return [lax.ppermute(b, axis, p) for b, p in zip(blocks, partners)]


def xor_trade(value, step):
    return lax.ppermute(value, "y", [(i, i ^ step) for i in range(SIZES["y"])])


def body(tokens, grad_out, w_gate, w_up, w_down):
    nx, ny = SIZES["x"], SIZES["y"]
    rows = w_gate.shape[0]
    t, d = tokens.shape
    x_partners = [[(i, (i + k) % nx) for i in range(nx)] for k in (1, nx - 1, 2)]
    w_down_t = w_down.T
    weights = []
    at = 0
    for width in WIDTHS:
        part = slice(at, at + width)
        at += width
        own = jnp.concatenate([w_gate[:, part], w_up[:, part], w_down_t[:, part]], axis=1)
        weights.append(lax.all_gather(own, "x", axis=0, tiled=True))
    x2, dy2 = gather_tokens(tokens, grad_out)
    rotor = hadamard(HB)
    me = lax.axis_index("x")

    half = 2 * t
    kept, fulls = [], []
    done = None
    for w, width in zip(weights, WIDTHS):
        w = after(w, done)
        cut = 2 * width
        sides = [(x2, w[:, :cut]), (dy2, w[:, cut:])]
        give = [dot(v[half:], u, ((1,), (0,))).astype(BF) for v, u in sides]
        got = xor_trade(jnp.concatenate(give, axis=1), 1)
        got = [got[:, :cut], got[:, cut:]]
        keep = [dot(v[:half], u, ((1,), (0,))) for v, u in sides]
        keep = [k + g.astype(F32) for k, g in zip(keep, got)]
        done = jnp.concatenate([k.astype(BF) for k in keep], axis=1)
        done = jnp.concatenate([done[t:], done[:t]], axis=0)
        kept.append((keep, xor_trade(done, 2)))

    for ((gu, d_hidden), got), width in zip(kept, WIDTHS):
        gu = gu + got[:, : 2 * width].astype(F32)
        d_hidden = d_hidden + got[:, 2 * width :].astype(F32)
        gate, up = gu[:, :width], gu[:, width:]
        sig = jax.nn.sigmoid(gate)
        active = gate * sig
        hidden = (active * up).astype(BF)
        d_gate = (d_hidden * up * sig * (1.0 + gate * (1.0 - sig))).astype(BF)
        d_up = (d_hidden * active).astype(BF)
        mine = jnp.concatenate([d_gate, d_up, hidden], axis=1)
        fulls.append(jnp.concatenate([mine, xor_trade(mine, 1)], axis=0))

    def columns(v, step):
        return lax.dynamic_slice_in_dim(v, lax.rem(me + step, nx) * rows, rows, axis=1)

    steps = (0, 1, nx - 1, 2)
    x_cols = [columns(x2, s) for s in steps]
    dy_cols = [columns(dy2, s) for s in steps]

    first = lax.axis_index("c") == 0

    def core_rows(w, own):
        w = w.reshape(-1, 2, d, w.shape[1])
        return jnp.where(first == own, w[:, 0], w[:, 1]).reshape(-1, w.shape[-1])

    sums = []
    give = keep = 0.0
    done = None
    for full, w, width in zip(fulls, weights, WIDTHS):
        full = after(full, done)
        dgu, hid = full[:, : 2 * width], full[:, 2 * width :]
        give = give + dot(dgu, core_rows(w[:, : 2 * width], False), ((1,), (1,)))
        last = len(sums) == len(WIDTHS) - 1
        if last:
            dgu, hid = after((dgu, hid), give)

        def piece(k):
            return jnp.concatenate(
                [dot(x_cols[k], dgu, ((0,), (0,))), dot(dy_cols[k], hid, ((0,), (0,)))], axis=1
            )

        send = [piece(k).astype(BF) for k in range(1, nx)]
        got = trade(send[:1], "x", x_partners)
        done = got
        keep = keep + dot(dgu, core_rows(w[:, : 2 * width], True), ((1,), (1,)))
        got = got + trade(send[1:], "x", x_partners[1:])
        sums.append((piece(0), got))
    pieces = (keep + other_core(give)).astype(BF).reshape(ny, t, -1, d)
    pieces = pieces.transpose(0, 2, 1, 3).reshape(-1, t, d)
    late = sum_first(swap_all_to_all(pieces, ("z", "h"))).astype(BF)
    grad_tokens = lax.ppermute(late, EVERY, exchange_pairs(0, True))

    gates, ups, downs = [], [], []
    for (gw, got), width in zip(sums, WIDTHS):
        gw = after(gw, (late, gates, ups, downs) if gates else pieces)
        for g in got:
            gw = gw + g.astype(F32)
        gw = gw.reshape(rows // HB, HB, 3 * width)
        rot = jnp.einsum(
            "ij,bjf->bif", rotor, gw[:, :, : 2 * width], precision=lax.Precision.HIGHEST
        ).astype(BF)
        rot = rot.reshape(rows, 2 * width)
        gates.append(rot[:, :width])
        ups.append(rot[:, width:])
        downs.append(
            jnp.einsum(
                "bjf,ij->fbi", gw[:, :, 2 * width :], rotor, precision=lax.Precision.HIGHEST
            )
            .reshape(width, rows)
            .astype(BF)
        )
    return (
        grad_tokens,
        jnp.concatenate(gates, axis=1),
        jnp.concatenate(ups, axis=1),
        jnp.concatenate(downs, axis=0),
    )


def solution(mesh):
    fine = Mesh(mesh.devices.reshape(tuple(SIZES[a] for a in EVERY)), EVERY)
    return jax.shard_map(
        body,
        mesh=fine,
        in_specs=(P(FSDP, REP), P(FSDP, REP), P(FSDP, REP), P(FSDP, REP), P(REP, FSDP)),
        out_specs=(P(FSDP, REP), P(FSDP, REP), P(FSDP, REP), P(REP, FSDP)),
        check_vma=False,
    )
```

```python
import functools
import math

import jax
import jax.numpy as jnp
from jax import lax
from jax.experimental import pallas as pl
from jax.experimental.pallas import tpu as pltpu
from jax.sharding import Mesh
from jax.sharding import PartitionSpec as P

HB = 128
WIDTHS = (384, 384)
SIZES = {"z": 8, "h": 2, "c": 2, "y": 4, "x": 4}
EVERY = ("z", "h", "c", "y", "x")
REP = ("z", "h", "c")
FSDP = ("y", "x")
BF = jnp.bfloat16
F32 = jnp.float32


def hadamard(size):
    index = jnp.arange(size, dtype=jnp.int32)
    both = index[:, None] & index[None, :]
    parity = jnp.zeros((size, size), jnp.int32)
    for bit_pos in range(size.bit_length() - 1):
        parity = parity + (both >> bit_pos & 1)
    return (1 - 2 * (parity % 2)).astype(F32) / math.sqrt(size)


ORDER = (0, 2, 1, 3)


def exchange_pairs(flip, back=False):
    nz, nh, nc, ny, nx = (SIZES[a] for a in EVERY)
    pairs = []
    for z in range(nz):
        for h in range(nh):
            for c in range(nc):
                for y in range(ny):
                    for x in range(nx):
                        src = (((z * nh + h) * nc + c) * ny + y) * nx + x
                        yy, hh = z // 2, h ^ flip
                        zz = 2 * ORDER[y ^ yy] + z % 2
                        dst = (((zz * nh + hh) * nc + c) * ny + yy) * nx + x
                        pairs.append((dst, src) if back else (src, dst))
    return pairs


def dot(left, right, dims):
    return lax.dot_general(left, right, (dims, ((), ())), preferred_element_type=F32)


def swap_all_to_all(value, axes):
    return lax.all_to_all(value, axes, split_axis=0, concat_axis=0, tiled=True)


def sum_first(value):
    terms = [value[i].astype(F32) for i in range(value.shape[0])]
    while len(terms) > 1:
        terms = [a + b for a, b in zip(terms[::2], terms[1::2])]
    return terms[0]


def other_core(value):
    return lax.ppermute(value, "c", [(0, 1), (1, 0)])


def place_blocks(core, mine, theirs, x_out, dy_out):
    t, d = mine.shape[-2:]
    for source, c in ((mine, core[0]), (theirs, 1 - core[0])):
        for z in range(mine.shape[0]):
            for h in range(2):
                at = pl.ds(pl.multiple_of((((z % 2) * 2 + h) * 2 + c) * d, d), d)
                for s, out in enumerate((x_out, dy_out)):
                    out[pl.ds(z // 2 * t, t), at] = source[z, h, s]


def gather_tokens(tokens, grad_out):
    nz, ny = SIZES["z"], SIZES["y"]
    t, d = tokens.shape
    both = jnp.stack([tokens, grad_out])
    mine = lax.ppermute(both, EVERY, exchange_pairs(0))
    far = lax.ppermute(both, EVERY, exchange_pairs(1))
    low = lax.axis_index("h") == 0
    pair = jnp.stack([jnp.where(low, mine, far), jnp.where(low, far, mine)])
    one = swap_all_to_all(jnp.broadcast_to(pair[None], (nz,) + pair.shape), "z")
    shape = jax.ShapeDtypeStruct((ny * t, d * nz), BF)
    vmem = pl.BlockSpec(memory_space=pltpu.VMEM)
    return pl.pallas_call(
        place_blocks,
        out_shape=(shape, shape),
        in_specs=[pl.BlockSpec(memory_space=pltpu.SMEM), vmem, vmem],
        out_specs=(vmem, vmem),
        compiler_params=pltpu.CompilerParams(vmem_limit_bytes=16 * 2**20),
        cost_estimate=pl.CostEstimate(flops=0, bytes_accessed=2**22, transcendentals=0),
    )(lax.axis_index("c").astype(jnp.int32)[None], one, other_core(one))


def x_blocks(width, me, x_rows, dy_rows, top, low, *outs):
    nx = SIZES["x"]
    rows = outs[0].shape[0]
    for out, step in zip(outs, (1, nx - 1, 2)):
        at = pl.ds(pl.multiple_of(lax.rem(me[0] + step, nx) * rows, rows), rows)
        for lhs, lo, hi in ((x_rows, 0, 2 * width), (dy_rows, 2 * width, 3 * width)):
            half = top.shape[0]
            block = dot(lhs[at, :half], top[:, lo:hi], ((1,), (0,)))
            block += dot(lhs[at, half:], low[:, lo:hi], ((1,), (0,)))
            out[:, lo:hi] = block.astype(BF)


def blocks_to_send(me, x_rows, dy_rows, top, low, rows):
    width = top.shape[1] // 3
    vmem = pl.BlockSpec(memory_space=pltpu.VMEM)
    count = SIZES["x"] - 1
    return list(
        pl.pallas_call(
            functools.partial(x_blocks, width),
            out_shape=(jax.ShapeDtypeStruct((rows, 3 * width), BF),) * count,
            in_specs=[pl.BlockSpec(memory_space=pltpu.SMEM), vmem, vmem, vmem, vmem],
            out_specs=(vmem,) * count,
            compiler_params=pltpu.CompilerParams(vmem_limit_bytes=24 * 2**20),
            cost_estimate=pl.CostEstimate(
                flops=4 * count * rows * top.size, bytes_accessed=2**22, transcendentals=0
            ),
        )(me.astype(jnp.int32)[None], x_rows, dy_rows, top, low)
    )


def after(value, others):
    return value if others is None else lax.optimization_barrier((value, others))[0]


def trade(blocks, axis, partners):
    return [lax.ppermute(b, axis, p) for b, p in zip(blocks, partners)]


def xor_trade(value, step):
    return lax.ppermute(value, "y", [(i, i ^ step) for i in range(SIZES["y"])])


def body(tokens, grad_out, w_gate, w_up, w_down):
    nx, ny = SIZES["x"], SIZES["y"]
    rows = w_gate.shape[0]
    t, d = tokens.shape
    x_partners = [[(i, (i + k) % nx) for i in range(nx)] for k in (1, nx - 1, 2)]
    w_down_t = w_down.T
    weights = []
    at = 0
    for width in WIDTHS:
        part = slice(at, at + width)
        at += width
        own = jnp.concatenate([w_gate[:, part], w_up[:, part], w_down_t[:, part]], axis=1)
        weights.append(lax.all_gather(own, "x", axis=0, tiled=True))
    x2, dy2 = gather_tokens(tokens, grad_out)
    rotor = hadamard(HB)
    me = lax.axis_index("x")

    half = 2 * t
    turned = [x2.T, dy2.T]
    kept, fulls = [], []
    done = None
    for w, width in zip(weights, WIDTHS):
        w = after(w, done)
        cut = 2 * width
        sides = [(x2, w[:, :cut]), (dy2, w[:, cut:])]
        give = [dot(v[half:], u, ((1,), (0,))).astype(BF) for v, u in sides]
        got = xor_trade(jnp.concatenate(give, axis=1), 1)
        if not kept:
            got = after(got, turned)
        got = [got[:, :cut], got[:, cut:]]
        keep = [dot(v[:half], u, ((1,), (0,))) for v, u in sides]
        keep = [k + g.astype(F32) for k, g in zip(keep, got)]
        done = jnp.concatenate([k.astype(BF) for k in keep], axis=1)
        done = jnp.concatenate([done[t:], done[:t]], axis=0)
        kept.append((keep, xor_trade(done, 2)))

    for ((gu, d_hidden), got), width in zip(kept, WIDTHS):
        gu = gu + got[:, : 2 * width].astype(F32)
        d_hidden = d_hidden + got[:, 2 * width :].astype(F32)
        gate, up = gu[:, :width], gu[:, width:]
        sig = jax.nn.sigmoid(gate)
        active = gate * sig
        hidden = (active * up).astype(BF)
        d_gate = (d_hidden * up * sig * (1.0 + gate * (1.0 - sig))).astype(BF)
        d_up = (d_hidden * active).astype(BF)
        mine = jnp.concatenate([d_gate, d_up, hidden], axis=1)
        fulls.append((mine, xor_trade(mine, 1)))

    x_cols, dy_cols = [
        lax.dynamic_slice_in_dim(v, me * rows, rows, axis=1) for v in (x2, dy2)
    ]

    first = lax.axis_index("c") == 0

    def core_rows(w, own):
        w = w.reshape(-1, 2, d, w.shape[1])
        return jnp.where(first == own, w[:, 0], w[:, 1]).reshape(-1, w.shape[-1])

    sums = []
    give, keep = [0.0, 0.0], [0.0, 0.0]
    done = None
    for halves, w, width in zip(fulls, weights, WIDTHS):
        last = len(sums) == len(WIDTHS) - 1
        w_give, w_keep = [core_rows(w[:, : 2 * width], own) for own in (False, True)]

        def add(i, part):
            part = part[:, : 2 * width]
            give[i] = give[i] + dot(part, w_give, ((1,), (1,)))
            keep[i] = keep[i] + dot(part, w_keep, ((1,), (1,)))

        mine, low = halves
        add(0, mine)
        if last:
            top = (keep[0] + other_core(give[0])).astype(BF)
            low = after(low, top)
        low = after(low, done)
        add(1, low)
        if last:
            low = after(low, give[1])
        send = blocks_to_send(me, *turned, mine, low, rows)
        got = trade(send, "x", x_partners)
        done = got[:1]
        if last:
            bottom = (keep[1] + other_core(give[1])).astype(BF)
            pieces = jnp.concatenate([top, bottom], axis=0).reshape(ny, t, -1, d)
            pieces = pieces.transpose(0, 2, 1, 3).reshape(-1, t, d)
            low = after(low, pieces)
        half = 2 * t
        own = [
            dot(v[:half], mine[:, lo:hi], ((0,), (0,)))
            + dot(v[half:], low[:, lo:hi], ((0,), (0,)))
            for v, lo, hi in ((x_cols, 0, 2 * width), (dy_cols, 2 * width, 3 * width))
        ]
        sums.append((jnp.concatenate(own, axis=1), got))
    late = sum_first(swap_all_to_all(pieces, ("z", "h"))).astype(BF)
    grad_tokens = lax.ppermute(late, EVERY, exchange_pairs(0, True))

    gates, ups, downs = [], [], []
    for (gw, got), width in zip(sums, WIDTHS):
        gw = after(gw, (late, gates, ups, downs) if gates else pieces)
        for g in got:
            gw = gw + g.astype(F32)
        gw = gw.reshape(rows // HB, HB, 3 * width)
        rot = jnp.einsum(
            "ij,bjf->bif", rotor, gw[:, :, : 2 * width], precision=lax.Precision.HIGHEST
        ).astype(BF)
        rot = rot.reshape(rows, 2 * width)
        gates.append(rot[:, :width])
        ups.append(rot[:, width:])
        downs.append(
            jnp.einsum(
                "bjf,ij->fbi", gw[:, :, 2 * width :], rotor, precision=lax.Precision.HIGHEST
            )
            .reshape(width, rows)
            .astype(BF)
        )
    return (
        grad_tokens,
        jnp.concatenate(gates, axis=1),
        jnp.concatenate(ups, axis=1),
        jnp.concatenate(downs, axis=0),
    )


def solution(mesh):
    fine = Mesh(mesh.devices.reshape(tuple(SIZES[a] for a in EVERY)), EVERY)
    return jax.shard_map(
        body,
        mesh=fine,
        in_specs=(P(FSDP, REP), P(FSDP, REP), P(FSDP, REP), P(FSDP, REP), P(REP, FSDP)),
        out_specs=(P(FSDP, REP), P(FSDP, REP), P(FSDP, REP), P(REP, FSDP)),
        check_vma=False,
    )
```

```python
import functools
import math

import jax
import jax.numpy as jnp
from jax import lax
from jax.experimental import pallas as pl
from jax.experimental.pallas import tpu as pltpu
from jax.sharding import Mesh
from jax.sharding import PartitionSpec as P

HB = 128
WIDTHS = (384, 384)
SIZES = {"z": 8, "h": 2, "c": 2, "y": 4, "x": 4}
EVERY = ("z", "h", "c", "y", "x")
REP = ("z", "h", "c")
FSDP = ("y", "x")
BF = jnp.bfloat16
F32 = jnp.float32


def hadamard(size):
    index = jnp.arange(size, dtype=jnp.int32)
    both = index[:, None] & index[None, :]
    parity = jnp.zeros((size, size), jnp.int32)
    for bit_pos in range(size.bit_length() - 1):
        parity = parity + (both >> bit_pos & 1)
    return (1 - 2 * (parity % 2)).astype(F32) / math.sqrt(size)


ORDER = (0, 2, 1, 3)


def exchange_pairs(flip, back=False):
    nz, nh, nc, ny, nx = (SIZES[a] for a in EVERY)
    pairs = []
    for z in range(nz):
        for h in range(nh):
            for c in range(nc):
                for y in range(ny):
                    for x in range(nx):
                        src = (((z * nh + h) * nc + c) * ny + y) * nx + x
                        yy, hh = z // 2, h ^ flip
                        zz = 2 * ORDER[y ^ yy] + z % 2
                        dst = (((zz * nh + hh) * nc + c) * ny + yy) * nx + x
                        pairs.append((dst, src) if back else (src, dst))
    return pairs


def dot(left, right, dims):
    return lax.dot_general(left, right, (dims, ((), ())), preferred_element_type=F32)


def swap_all_to_all(value, axes):
    return lax.all_to_all(value, axes, split_axis=0, concat_axis=0, tiled=True)


def sum_first(value):
    terms = [value[i].astype(F32) for i in range(value.shape[0])]
    while len(terms) > 1:
        terms = [a + b for a, b in zip(terms[::2], terms[1::2])]
    return terms[0]


def other_core(value):
    return lax.ppermute(value, "c", [(0, 1), (1, 0)])


def place_blocks(core, mine, theirs, x_out, dy_out):
    t, d = mine.shape[-2:]
    for source, c in ((mine, core[0]), (theirs, 1 - core[0])):
        for z in range(mine.shape[0]):
            for h in range(2):
                at = pl.ds(pl.multiple_of((((z % 2) * 2 + h) * 2 + c) * d, d), d)
                for s, out in enumerate((x_out, dy_out)):
                    out[pl.ds(z // 2 * t, t), at] = source[z, h, s]


def gather_tokens(tokens, grad_out):
    nz, ny = SIZES["z"], SIZES["y"]
    t, d = tokens.shape
    both = jnp.stack([tokens, grad_out])
    mine = lax.ppermute(both, EVERY, exchange_pairs(0))
    far = lax.ppermute(both, EVERY, exchange_pairs(1))
    low = lax.axis_index("h") == 0
    pair = jnp.stack([jnp.where(low, mine, far), jnp.where(low, far, mine)])
    one = swap_all_to_all(jnp.broadcast_to(pair[None], (nz,) + pair.shape), "z")
    shape = jax.ShapeDtypeStruct((ny * t, d * nz), BF)
    vmem = pl.BlockSpec(memory_space=pltpu.VMEM)
    return pl.pallas_call(
        place_blocks,
        out_shape=(shape, shape),
        in_specs=[pl.BlockSpec(memory_space=pltpu.SMEM), vmem, vmem],
        out_specs=(vmem, vmem),
        compiler_params=pltpu.CompilerParams(vmem_limit_bytes=16 * 2**20),
        cost_estimate=pl.CostEstimate(flops=0, bytes_accessed=2**22, transcendentals=0),
    )(lax.axis_index("c").astype(jnp.int32)[None], one, other_core(one))


def x_blocks(width, me, x_rows, dy_rows, top, low, *outs):
    nx = SIZES["x"]
    rows = outs[0].shape[0]
    for out, step in zip(outs, (1, nx - 1, 2)):
        at = pl.ds(pl.multiple_of(lax.rem(me[0] + step, nx) * rows, rows), rows)
        for lhs, lo, hi in ((x_rows, 0, 2 * width), (dy_rows, 2 * width, 3 * width)):
            half = top.shape[0]
            block = dot(lhs[at, :half], top[:, lo:hi], ((1,), (0,)))
            block += dot(lhs[at, half:], low[:, lo:hi], ((1,), (0,)))
            out[:, lo:hi] = block.astype(BF)


def blocks_to_send(me, x_rows, dy_rows, top, low, rows):
    width = top.shape[1] // 3
    vmem = pl.BlockSpec(memory_space=pltpu.VMEM)
    count = SIZES["x"] - 1
    return list(
        pl.pallas_call(
            functools.partial(x_blocks, width),
            out_shape=(jax.ShapeDtypeStruct((rows, 3 * width), BF),) * count,
            in_specs=[pl.BlockSpec(memory_space=pltpu.SMEM), vmem, vmem, vmem, vmem],
            out_specs=(vmem,) * count,
            compiler_params=pltpu.CompilerParams(vmem_limit_bytes=24 * 2**20),
            cost_estimate=pl.CostEstimate(
                flops=4 * count * rows * top.size, bytes_accessed=2**22, transcendentals=0
            ),
        )(me.astype(jnp.int32)[None], x_rows, dy_rows, top, low)
    )


def after(value, others):
    return value if others is None else lax.optimization_barrier((value, others))[0]


def trade(blocks, axis, partners):
    return [lax.ppermute(b, axis, p) for b, p in zip(blocks, partners)]


def xor_trade(value, step):
    return lax.ppermute(value, "y", [(i, i ^ step) for i in range(SIZES["y"])])


def body(tokens, grad_out, w_gate, w_up, w_down):
    nx, ny = SIZES["x"], SIZES["y"]
    rows = w_gate.shape[0]
    t, d = tokens.shape
    x_partners = [[(i, (i + k) % nx) for i in range(nx)] for k in (1, nx - 1, 2)]
    w_down_t = w_down.T
    weights = []
    at = 0
    for width in WIDTHS:
        part = slice(at, at + width)
        at += width
        own = jnp.concatenate([w_gate[:, part], w_up[:, part], w_down_t[:, part]], axis=1)
        weights.append(lax.all_gather(own, "x", axis=0, tiled=True))
    x2, dy2 = gather_tokens(tokens, grad_out)
    rotor = hadamard(HB)
    me = lax.axis_index("x")

    half = 2 * t
    kept, fulls = [], []
    done = None
    for w, width in zip(weights, WIDTHS):
        w = after(w, done)
        cut = 2 * width
        sides = [(x2, w[:, :cut]), (dy2, w[:, cut:])]
        give = [dot(v[half:], u, ((1,), (0,))).astype(BF) for v, u in sides]
        got = xor_trade(jnp.concatenate(give, axis=1), 1)
        got = [got[:, :cut], got[:, cut:]]
        keep = [dot(v[:half], u, ((1,), (0,))) for v, u in sides]
        keep = [k + g.astype(F32) for k, g in zip(keep, got)]
        done = jnp.concatenate([k.astype(BF) for k in keep], axis=1)
        done = jnp.concatenate([done[t:], done[:t]], axis=0)
        kept.append((keep, xor_trade(done, 2)))

    for ((gu, d_hidden), got), width in zip(kept, WIDTHS):
        gu = gu + got[:, : 2 * width].astype(F32)
        d_hidden = d_hidden + got[:, 2 * width :].astype(F32)
        gate, up = gu[:, :width], gu[:, width:]
        sig = jax.nn.sigmoid(gate)
        active = gate * sig
        hidden = (active * up).astype(BF)
        d_gate = (d_hidden * up * sig * (1.0 + gate * (1.0 - sig))).astype(BF)
        d_up = (d_hidden * active).astype(BF)
        mine = jnp.concatenate([d_gate, d_up, hidden], axis=1)
        fulls.append((mine, xor_trade(mine, 1)))

    def columns(v, step):
        return lax.dynamic_slice_in_dim(v, lax.rem(me + step, nx) * rows, rows, axis=1)

    steps = (0, 1, nx - 1, 2)
    turned = [x2.T, dy2.T]
    x_cols = [columns(x2, s) for s in steps]
    dy_cols = [columns(dy2, s) for s in steps]

    first = lax.axis_index("c") == 0

    def core_rows(w, own):
        w = w.reshape(-1, 2, d, w.shape[1])
        return jnp.where(first == own, w[:, 0], w[:, 1]).reshape(-1, w.shape[-1])

    sums = []
    give = keep = 0.0
    done = None
    for full, w, width in zip(fulls, weights, WIDTHS):
        mine, low = full
        low = after(low, done)
        full = jnp.concatenate([mine, low], axis=0)
        dgu, hid = full[:, : 2 * width], full[:, 2 * width :]
        give = give + dot(dgu, core_rows(w[:, : 2 * width], False), ((1,), (1,)))
        last = len(sums) == len(WIDTHS) - 1
        if last:
            dgu, hid = after((dgu, hid), give)

        def piece(k):
            return jnp.concatenate(
                [dot(x_cols[k], dgu, ((0,), (0,))), dot(dy_cols[k], hid, ((0,), (0,)))], axis=1
            )

        if last:
            send = blocks_to_send(me, *turned, mine, after(low, give), rows)
        else:
            send = [piece(k).astype(BF) for k in range(1, nx)]
        got = trade(send[:1], "x", x_partners)
        done = got
        keep = keep + dot(dgu, core_rows(w[:, : 2 * width], True), ((1,), (1,)))
        got = got + trade(send[1:], "x", x_partners[1:])
        if last:
            pieces = (keep + other_core(give)).astype(BF).reshape(ny, t, -1, d)
            pieces = pieces.transpose(0, 2, 1, 3).reshape(-1, t, d)
            dgu, hid = after((dgu, hid), pieces)
        sums.append((piece(0), got))
    late = sum_first(swap_all_to_all(pieces, ("z", "h"))).astype(BF)
    grad_tokens = lax.ppermute(late, EVERY, exchange_pairs(0, True))

    gates, ups, downs = [], [], []
    for (gw, got), width in zip(sums, WIDTHS):
        gw = after(gw, (late, gates, ups, downs) if gates else pieces)
        for g in got:
            gw = gw + g.astype(F32)
        gw = gw.reshape(rows // HB, HB, 3 * width)
        rot = jnp.einsum(
            "ij,bjf->bif", rotor, gw[:, :, : 2 * width], precision=lax.Precision.HIGHEST
        ).astype(BF)
        rot = rot.reshape(rows, 2 * width)
        gates.append(rot[:, :width])
        ups.append(rot[:, width:])
        downs.append(
            jnp.einsum(
                "bjf,ij->fbi", gw[:, :, 2 * width :], rotor, precision=lax.Precision.HIGHEST
            )
            .reshape(width, rows)
            .astype(BF)
        )
    return (
        grad_tokens,
        jnp.concatenate(gates, axis=1),
        jnp.concatenate(ups, axis=1),
        jnp.concatenate(downs, axis=0),
    )


def solution(mesh):
    fine = Mesh(mesh.devices.reshape(tuple(SIZES[a] for a in EVERY)), EVERY)
    return jax.shard_map(
        body,
        mesh=fine,
        in_specs=(P(FSDP, REP), P(FSDP, REP), P(FSDP, REP), P(FSDP, REP), P(REP, FSDP)),
        out_specs=(P(FSDP, REP), P(FSDP, REP), P(FSDP, REP), P(REP, FSDP)),
        check_vma=False,
    )
```

```python
import math

import jax
import jax.numpy as jnp
from jax import lax
from jax.experimental import pallas as pl
from jax.experimental.pallas import tpu as pltpu
from jax.sharding import Mesh
from jax.sharding import PartitionSpec as P

HB = 128
WIDTHS = (384, 384)
SIZES = {"z": 8, "h": 2, "c": 2, "y": 4, "x": 4}
EVERY = ("z", "h", "c", "y", "x")
REP = ("z", "h", "c")
FSDP = ("y", "x")
BF = jnp.bfloat16
F32 = jnp.float32


def hadamard(size):
    index = jnp.arange(size, dtype=jnp.int32)
    both = index[:, None] & index[None, :]
    parity = jnp.zeros((size, size), jnp.int32)
    for bit_pos in range(size.bit_length() - 1):
        parity = parity + (both >> bit_pos & 1)
    return (1 - 2 * (parity % 2)).astype(F32) / math.sqrt(size)


ORDER = (0, 2, 1, 3)


def exchange_pairs(flip, back=False):
    nz, nh, nc, ny, nx = (SIZES[a] for a in EVERY)
    pairs = []
    for z in range(nz):
        for h in range(nh):
            for c in range(nc):
                for y in range(ny):
                    for x in range(nx):
                        src = (((z * nh + h) * nc + c) * ny + y) * nx + x
                        yy, hh = z // 2, h ^ flip
                        zz = 2 * ORDER[y ^ yy] + z % 2
                        dst = (((zz * nh + hh) * nc + c) * ny + yy) * nx + x
                        pairs.append((dst, src) if back else (src, dst))
    return pairs


def dot(left, right, dims):
    return lax.dot_general(left, right, (dims, ((), ())), preferred_element_type=F32)


def swap_all_to_all(value, axes):
    return lax.all_to_all(value, axes, split_axis=0, concat_axis=0, tiled=True)


def sum_first(value):
    terms = [value[i].astype(F32) for i in range(value.shape[0])]
    while len(terms) > 1:
        terms = [a + b for a, b in zip(terms[::2], terms[1::2])]
    return terms[0]


def other_core(value):
    return lax.ppermute(value, "c", [(0, 1), (1, 0)])


def place_blocks(core, mine, theirs, x_out, dy_out):
    t, d = mine.shape[-2:]
    for source, c in ((mine, core[0]), (theirs, 1 - core[0])):
        for z in range(mine.shape[0]):
            for h in range(2):
                at = pl.ds(pl.multiple_of((((z % 2) * 2 + h) * 2 + c) * d, d), d)
                for s, out in enumerate((x_out, dy_out)):
                    out[pl.ds(z // 2 * t, t), at] = source[z, h, s]


def gather_tokens(tokens, grad_out):
    nz, ny = SIZES["z"], SIZES["y"]
    t, d = tokens.shape
    both = jnp.stack([tokens, grad_out])
    mine = lax.ppermute(both, EVERY, exchange_pairs(0))
    far = lax.ppermute(both, EVERY, exchange_pairs(1))
    low = lax.axis_index("h") == 0
    pair = jnp.stack([jnp.where(low, mine, far), jnp.where(low, far, mine)])
    one = swap_all_to_all(jnp.broadcast_to(pair[None], (nz,) + pair.shape), "z")
    shape = jax.ShapeDtypeStruct((ny * t, d * nz), BF)
    vmem = pl.BlockSpec(memory_space=pltpu.VMEM)
    return pl.pallas_call(
        place_blocks,
        out_shape=(shape, shape),
        in_specs=[pl.BlockSpec(memory_space=pltpu.SMEM), vmem, vmem],
        out_specs=(vmem, vmem),
        compiler_params=pltpu.CompilerParams(vmem_limit_bytes=16 * 2**20),
        cost_estimate=pl.CostEstimate(flops=0, bytes_accessed=2**22, transcendentals=0),
    )(lax.axis_index("c").astype(jnp.int32)[None], one, other_core(one))


def after(value, others):
    return value if others is None else lax.optimization_barrier((value, others))[0]


def trade(blocks, axis, partners):
    return [lax.ppermute(b, axis, p) for b, p in zip(blocks, partners)]


def xor_trade(value, step):
    return lax.ppermute(value, "y", [(i, i ^ step) for i in range(SIZES["y"])])


def body(tokens, grad_out, w_gate, w_up, w_down):
    nx, ny = SIZES["x"], SIZES["y"]
    rows = w_gate.shape[0]
    t, d = tokens.shape
    x_partners = [[(i, (i + k) % nx) for i in range(nx)] for k in (1, nx - 1, 2)]
    w_down_t = w_down.T
    weights = []
    at = 0
    for width in WIDTHS:
        part = slice(at, at + width)
        at += width
        own = jnp.concatenate([w_gate[:, part], w_up[:, part], w_down_t[:, part]], axis=1)
        weights.append(lax.all_gather(own, "x", axis=0, tiled=True))
    x2, dy2 = gather_tokens(tokens, grad_out)
    rotor = hadamard(HB)
    me = lax.axis_index("x")

    half = 2 * t
    kept, fulls = [], []
    done = None
    for w, width in zip(weights, WIDTHS):
        w = after(w, done)
        cut = 2 * width
        sides = [(x2, w[:, :cut]), (dy2, w[:, cut:])]
        give = [dot(v[half:], u, ((1,), (0,))).astype(BF) for v, u in sides]
        got = xor_trade(jnp.concatenate(give, axis=1), 1)
        got = [got[:, :cut], got[:, cut:]]
        keep = [dot(v[:half], u, ((1,), (0,))) for v, u in sides]
        keep = [k + g.astype(F32) for k, g in zip(keep, got)]
        done = jnp.concatenate([k.astype(BF) for k in keep], axis=1)
        done = jnp.concatenate([done[t:], done[:t]], axis=0)
        kept.append((keep, xor_trade(done, 2)))

    for ((gu, d_hidden), got), width in zip(kept, WIDTHS):
        gu = gu + got[:, : 2 * width].astype(F32)
        d_hidden = d_hidden + got[:, 2 * width :].astype(F32)
        gate, up = gu[:, :width], gu[:, width:]
        sig = jax.nn.sigmoid(gate)
        active = gate * sig
        hidden = (active * up).astype(BF)
        d_gate = (d_hidden * up * sig * (1.0 + gate * (1.0 - sig))).astype(BF)
        d_up = (d_hidden * active).astype(BF)
        mine = jnp.concatenate([d_gate, d_up, hidden], axis=1)
        fulls.append(jnp.concatenate([mine, xor_trade(mine, 1)], axis=0))

    def columns(v, step):
        return lax.dynamic_slice_in_dim(v, lax.rem(me + step, nx) * rows, rows, axis=1)

    steps = (0, 1, nx - 1, 2)
    x_cols = [columns(x2, s) for s in steps]
    dy_cols = [columns(dy2, s) for s in steps]

    first = lax.axis_index("c") == 0

    def core_rows(w, own):
        w = w.reshape(-1, 2, d, w.shape[1])
        return jnp.where(first == own, w[:, 0], w[:, 1]).reshape(-1, w.shape[-1])

    sums = []
    give = keep = 0.0
    done = None
    for full, w, width in zip(fulls, weights, WIDTHS):
        full = after(full, done)
        dgu, hid = full[:, : 2 * width], full[:, 2 * width :]
        give = give + dot(dgu, core_rows(w[:, : 2 * width], False), ((1,), (1,)))
        last = len(sums) == len(WIDTHS) - 1
        if last:
            dgu, hid = after((dgu, hid), give)

        def piece(k):
            return jnp.concatenate(
                [dot(x_cols[k], dgu, ((0,), (0,))), dot(dy_cols[k], hid, ((0,), (0,)))], axis=1
            )

        send = [piece(k).astype(BF) for k in range(1, nx)]
        got = trade(send[:1], "x", x_partners)
        done = got
        keep = keep + dot(dgu, core_rows(w[:, : 2 * width], True), ((1,), (1,)))
        got = got + trade(send[1:], "x", x_partners[1:])
        if last:
            pieces = (keep + other_core(give)).astype(BF).reshape(ny, t, -1, d)
            pieces = pieces.transpose(0, 2, 1, 3).reshape(-1, t, d)
            dgu, hid = after((dgu, hid), pieces)
        sums.append((piece(0), got))
    late = sum_first(swap_all_to_all(pieces, ("z", "h"))).astype(BF)
    grad_tokens = lax.ppermute(late, EVERY, exchange_pairs(0, True))

    gates, ups, downs = [], [], []
    for (gw, got), width in zip(sums, WIDTHS):
        gw = after(gw, (pieces, gates, ups, downs))
        for g in got:
            gw = gw + g.astype(F32)
        gw = gw.reshape(rows // HB, HB, 3 * width)
        rot = jnp.einsum(
            "ij,bjf->bif", rotor, gw[:, :, : 2 * width], precision=lax.Precision.HIGHEST
        ).astype(BF)
        rot = rot.reshape(rows, 2 * width)
        gates.append(rot[:, :width])
        ups.append(rot[:, width:])
        downs.append(
            jnp.einsum(
                "bjf,ij->fbi", gw[:, :, 2 * width :], rotor, precision=lax.Precision.HIGHEST
            )
            .reshape(width, rows)
            .astype(BF)
        )
    return (
        grad_tokens,
        jnp.concatenate(gates, axis=1),
        jnp.concatenate(ups, axis=1),
        jnp.concatenate(downs, axis=0),
    )


def solution(mesh):
    fine = Mesh(mesh.devices.reshape(tuple(SIZES[a] for a in EVERY)), EVERY)
    return jax.shard_map(
        body,
        mesh=fine,
        in_specs=(P(FSDP, REP), P(FSDP, REP), P(FSDP, REP), P(FSDP, REP), P(REP, FSDP)),
        out_specs=(P(FSDP, REP), P(FSDP, REP), P(FSDP, REP), P(REP, FSDP)),
        check_vma=False,
    )
```

```python
import math

import jax
import jax.numpy as jnp
from jax import lax
from jax.experimental import pallas as pl
from jax.experimental.pallas import tpu as pltpu
from jax.sharding import Mesh
from jax.sharding import PartitionSpec as P

HB = 128
WIDTHS = (384, 384)
SIZES = {"z": 8, "h": 2, "c": 2, "y": 4, "x": 4}
EVERY = ("z", "h", "c", "y", "x")
REP = ("z", "h", "c")
FSDP = ("y", "x")
BF = jnp.bfloat16
F32 = jnp.float32


def hadamard(size):
    index = jnp.arange(size, dtype=jnp.int32)
    both = index[:, None] & index[None, :]
    parity = jnp.zeros((size, size), jnp.int32)
    for bit_pos in range(size.bit_length() - 1):
        parity = parity + (both >> bit_pos & 1)
    return (1 - 2 * (parity % 2)).astype(F32) / math.sqrt(size)


ORDER = (0, 2, 1, 3)


def exchange_pairs(flip, back=False):
    nz, nh, nc, ny, nx = (SIZES[a] for a in EVERY)
    pairs = []
    for z in range(nz):
        for h in range(nh):
            for c in range(nc):
                for y in range(ny):
                    for x in range(nx):
                        src = (((z * nh + h) * nc + c) * ny + y) * nx + x
                        yy, hh = z // 2, h ^ flip
                        zz = 2 * ORDER[y ^ yy] + z % 2
                        dst = (((zz * nh + hh) * nc + c) * ny + yy) * nx + x
                        pairs.append((dst, src) if back else (src, dst))
    return pairs


def dot(left, right, dims):
    return lax.dot_general(left, right, (dims, ((), ())), preferred_element_type=F32)


def swap_all_to_all(value, axes):
    return lax.all_to_all(value, axes, split_axis=0, concat_axis=0, tiled=True)


def sum_first(value):
    terms = [value[i].astype(F32) for i in range(value.shape[0])]
    while len(terms) > 1:
        terms = [a + b for a, b in zip(terms[::2], terms[1::2])]
    return terms[0]


def other_core(value):
    return lax.ppermute(value, "c", [(0, 1), (1, 0)])


def place_blocks(core, mine, theirs, x_out, dy_out):
    t, d = mine.shape[-2:]
    for source, c in ((mine, core[0]), (theirs, 1 - core[0])):
        for z in range(mine.shape[0]):
            for h in range(2):
                at = pl.ds(pl.multiple_of((((z % 2) * 2 + h) * 2 + c) * d, d), d)
                for s, out in enumerate((x_out, dy_out)):
                    out[pl.ds(z // 2 * t, t), at] = source[z, h, s]


def gather_tokens(tokens, grad_out):
    nz, ny = SIZES["z"], SIZES["y"]
    t, d = tokens.shape
    both = jnp.stack([tokens, grad_out])
    mine = lax.ppermute(both, EVERY, exchange_pairs(0))
    far = lax.ppermute(both, EVERY, exchange_pairs(1))
    low = lax.axis_index("h") == 0
    pair = jnp.stack([jnp.where(low, mine, far), jnp.where(low, far, mine)])
    one = swap_all_to_all(jnp.broadcast_to(pair[None], (nz,) + pair.shape), "z")
    shape = jax.ShapeDtypeStruct((ny * t, d * nz), BF)
    vmem = pl.BlockSpec(memory_space=pltpu.VMEM)
    return pl.pallas_call(
        place_blocks,
        out_shape=(shape, shape),
        in_specs=[pl.BlockSpec(memory_space=pltpu.SMEM), vmem, vmem],
        out_specs=(vmem, vmem),
        compiler_params=pltpu.CompilerParams(vmem_limit_bytes=16 * 2**20),
        cost_estimate=pl.CostEstimate(flops=0, bytes_accessed=2**22, transcendentals=0),
    )(lax.axis_index("c").astype(jnp.int32)[None], one, other_core(one))


def after(value, others):
    return value if others is None else lax.optimization_barrier((value, others))[0]


def trade(blocks, axis, partners):
    return [lax.ppermute(b, axis, p) for b, p in zip(blocks, partners)]


def xor_trade(value, step):
    return lax.ppermute(value, "y", [(i, i ^ step) for i in range(SIZES["y"])])


def body(tokens, grad_out, w_gate, w_up, w_down):
    nx, ny = SIZES["x"], SIZES["y"]
    rows = w_gate.shape[0]
    t, d = tokens.shape
    x_partners = [[(i, (i + k) % nx) for i in range(nx)] for k in (1, nx - 1, 2)]
    w_down_t = w_down.T
    weights = []
    at = 0
    for width in WIDTHS:
        part = slice(at, at + width)
        at += width
        own = jnp.concatenate([w_gate[:, part], w_up[:, part], w_down_t[:, part]], axis=1)
        weights.append(lax.all_gather(own, "x", axis=0, tiled=True))
    x2, dy2 = gather_tokens(tokens, grad_out)
    rotor = hadamard(HB)
    me = lax.axis_index("x")

    half = 2 * t
    kept, fulls = [], []
    done = None
    for w, width in zip(weights, WIDTHS):
        w = after(w, done)
        cut = 2 * width
        sides = [(x2, w[:, :cut]), (dy2, w[:, cut:])]
        give = [dot(v[half:], u, ((1,), (0,))).astype(BF) for v, u in sides]
        got = xor_trade(jnp.concatenate(give, axis=1), 1)
        got = [got[:, :cut], got[:, cut:]]
        keep = [dot(v[:half], u, ((1,), (0,))) for v, u in sides]
        keep = [k + g.astype(F32) for k, g in zip(keep, got)]
        done = jnp.concatenate([k.astype(BF) for k in keep], axis=1)
        done = jnp.concatenate([done[t:], done[:t]], axis=0)
        kept.append((keep, xor_trade(done, 2)))

    for ((gu, d_hidden), got), width in zip(kept, WIDTHS):
        gu = gu + got[:, : 2 * width].astype(F32)
        d_hidden = d_hidden + got[:, 2 * width :].astype(F32)
        gate, up = gu[:, :width], gu[:, width:]
        sig = jax.nn.sigmoid(gate)
        active = gate * sig
        hidden = (active * up).astype(BF)
        d_gate = (d_hidden * up * sig * (1.0 + gate * (1.0 - sig))).astype(BF)
        d_up = (d_hidden * active).astype(BF)
        mine = jnp.concatenate([d_gate, d_up, hidden], axis=1)
        fulls.append(jnp.concatenate([mine, xor_trade(mine, 1)], axis=0))

    def columns(v, step):
        return lax.dynamic_slice_in_dim(v, lax.rem(me + step, nx) * rows, rows, axis=1)

    steps = (0, 1, nx - 1, 2)
    x_cols = [columns(x2, s) for s in steps]
    dy_cols = [columns(dy2, s) for s in steps]

    first = lax.axis_index("c") == 0

    def core_rows(w, own):
        w = w.reshape(-1, 2, d, w.shape[1])
        return jnp.where(first == own, w[:, 0], w[:, 1]).reshape(-1, w.shape[-1])

    sums = []
    give = keep = 0.0
    done = None
    for full, w, width in zip(fulls, weights, WIDTHS):
        full = after(full, done)
        dgu, hid = full[:, : 2 * width], full[:, 2 * width :]
        give = give + dot(dgu, core_rows(w[:, : 2 * width], False), ((1,), (1,)))
        last = len(sums) == len(WIDTHS) - 1
        if last:
            dgu, hid = after((dgu, hid), give)

        def piece(k):
            return jnp.concatenate(
                [dot(x_cols[k], dgu, ((0,), (0,))), dot(dy_cols[k], hid, ((0,), (0,)))], axis=1
            )

        send = [piece(k).astype(BF) for k in range(1, nx)]
        got = trade(send[:1], "x", x_partners)
        done = got
        keep = keep + dot(dgu, core_rows(w[:, : 2 * width], True), ((1,), (1,)))
        got = got + trade(send[1:], "x", x_partners[1:])
        sums.append((None if last else piece(0), got))
    pieces = (keep + other_core(give)).astype(BF).reshape(ny, t, -1, d)
    pieces = pieces.transpose(0, 2, 1, 3).reshape(-1, t, d)
    late = sum_first(swap_all_to_all(pieces, ("z", "h"))).astype(BF)
    grad_tokens = lax.ppermute(late, EVERY, exchange_pairs(0, True))

    dgu, hid = after((dgu, hid), late)
    sums[-1] = (piece(0), got)

    gates, ups, downs = [], [], []
    for (gw, got), width in zip(sums, WIDTHS):
        gw = after(gw, (late, gates, ups, downs) if gates else pieces)
        for g in got:
            gw = gw + g.astype(F32)
        gw = gw.reshape(rows // HB, HB, 3 * width)
        rot = jnp.einsum(
            "ij,bjf->bif", rotor, gw[:, :, : 2 * width], precision=lax.Precision.HIGHEST
        ).astype(BF)
        rot = rot.reshape(rows, 2 * width)
        gates.append(rot[:, :width])
        ups.append(rot[:, width:])
        downs.append(
            jnp.einsum(
                "bjf,ij->fbi", gw[:, :, 2 * width :], rotor, precision=lax.Precision.HIGHEST
            )
            .reshape(width, rows)
            .astype(BF)
        )
    return (
        grad_tokens,
        jnp.concatenate(gates, axis=1),
        jnp.concatenate(ups, axis=1),
        jnp.concatenate(downs, axis=0),
    )


def solution(mesh):
    fine = Mesh(mesh.devices.reshape(tuple(SIZES[a] for a in EVERY)), EVERY)
    return jax.shard_map(
        body,
        mesh=fine,
        in_specs=(P(FSDP, REP), P(FSDP, REP), P(FSDP, REP), P(FSDP, REP), P(REP, FSDP)),
        out_specs=(P(FSDP, REP), P(FSDP, REP), P(FSDP, REP), P(REP, FSDP)),
        check_vma=False,
    )
```
